512 devices in a mesh: ctx: 32 (over y_lo, z), tp: 4 (over x), dp: 4 (over y_hi, core).
Axes of the slice: x: 4, y: 4 (y_hi: 2, y_lo: 2; y = y_hi * 2 + y_lo), z: 16, core: 2. Of those that a mesh axis runs over, the one named last changes fastest.
Arguments:
- queries: bfloat16 [4, 4096, 4096], P('dp', 'ctx', 'tp'), may hold values from -6 to 6
- keys: bfloat16 [4, 32, 4, 32, 128, 128], P('dp', None, 'tp', 'ctx'), may hold values from -6 to 6
- values: bfloat16 [4, 32, 4, 32, 128, 128], P('dp', None, 'tp', 'ctx'), may hold values from -6 to 6
- cotangent: bfloat16 [4, 4096, 4096], P('dp', 'ctx', 'tp'), may hold values from -6 to 6
- lengths: int32 [4, 64, 2], P('dp'), may hold values from 16 to 128
Outputs:
- attended: bfloat16 [4, 4096, 4096], P('dp', 'ctx', 'tp')
- grad_queries: bfloat16 [4, 4096, 4096], P('dp', 'ctx', 'tp')
- grad_keys: bfloat16 [4, 32, 4, 32, 128, 128], P('dp', None, 'tp', 'ctx')
- grad_values: bfloat16 [4, 32, 4, 32, 128, 128], P('dp', None, 'tp', 'ctx')
The draws below stay inside these ranges and needn't reach their ends.
Inputs may be any that keep to these rules, and one draw needn't show every extreme that they name: Neighbour n of span u has its first lengths[u, n] tokens live; the others are padding.
All inputs are finite; a program needn't handle non-finite values.
Results may differ from the reference program's by a relative error of at most 0.012.
The reference program's roundings to bfloat16 on the way count: a program that leaves them out, or rounds other values in their place, can miss the bound.
Values may be sent and summed in bfloat16 or wider, within the bound.
No kernel may reach another device: no remote copies, remote signals or barrier semaphores. Data moves between devices by JAX's collectives and lax.ppermute only.
A program may use at most 64 MiB of HBM per device.

```python
import math
import jax
import jax.numpy as jnp
from jax import lax

HEADS = 32
DH = 128
SPAN = 64
NBR = 2
NEIGH = 128
TOK_DEV = 128
SEQ = 4096
SPANS = 64
PASS = 4
BATCH = 4
N_CTX = 32


def draw_queries(key, part):
    shape_all = (BATCH, SEQ, HEADS * DH)
    sampled = jnp.clip(jax.random.normal(key, shape_all, jnp.float32), -6.0, 6.0)
    return sampled.astype(jnp.bfloat16)


def draw_keys(key, part):
    block_count = SEQ // TOK_DEV
    shape_all = (BATCH, block_count, PASS, HEADS, NEIGH, DH)
    sampled = jnp.clip(jax.random.normal(jax.random.fold_in(key, 23), shape_all, jnp.float32), -6.0, 6.0)
    return sampled.astype(jnp.bfloat16)


def plant(drawn, rng, least, top_value):
    longest = drawn.shape.index(max(drawn.shape))
    spots = []
    for shift in (0, 1):
        where = [jax.random.randint(jax.random.fold_in(rng, axis), (), 0, length) for axis, length in enumerate(drawn.shape)]
        where[longest] = (where[longest] + shift) % drawn.shape[longest]
        spots.append(tuple(where))
    return drawn.at[spots[0]].set(least).at[spots[1]].set(top_value)


def steps_of(rng, dims, cuts, smallest, high):
    def one(position, parts):
        draws = jax.random.uniform(jax.random.fold_in(jax.random.fold_in(rng, 6), position), (parts,), jnp.float32, smallest / len(cuts), high / len(cuts))
        return jnp.repeat(jnp.exp(draws), dims[position] // parts).reshape((-1,) + (1,) * (len(dims) - position - 1))

    loudness = one(*cuts[0])
    for cut in cuts[1:]:
        loudness = loudness * one(*cut)
    return loudness


def scatter_about(stream_key, shape, scale, most, cuts=(), held_as=jnp.bfloat16):
    gain = steps_of(stream_key, shape, cuts, -0.22, 0.18) if cuts else 1.0
    drawn = jax.random.normal(stream_key, shape, jnp.float32) * scale * gain
    return jnp.minimum(jnp.maximum(drawn, -most), most).astype(held_as)


def setup_inputs(seed: int = 0) -> dict:
    seeds = jax.random.split(jax.random.key(seed), 6)
    queries = draw_queries(jax.random.fold_in(seeds[5], 71), 0)
    keys = draw_keys(jax.random.fold_in(seeds[5], 71), 0)
    values = scatter_about(seeds[2], (BATCH, N_CTX, PASS, HEADS, NEIGH, DH), 1.0, 6.0, ((0, 4), (2, 4), (3, 32)))
    cotangent = scatter_about(seeds[3], (BATCH, SEQ, HEADS * DH), 1.0, 6.0, ((0, 4), (1, 32), (2, 4)))
    lengths = plant(jax.random.randint(seeds[4], (BATCH, SPANS, NBR), NEIGH // 8, NEIGH + 1), jax.random.fold_in(seeds[4], 1), NEIGH // 8, NEIGH).astype(jnp.int32)
    return dict(queries=queries, keys=keys, values=values, cotangent=cotangent, lengths=lengths)


def rotate(tensor, direction):
    middle = tensor.shape[-1] // 2
    frequency = 10000.0 ** (-2.0 * jnp.arange(middle, dtype=jnp.float32) / tensor.shape[-1])
    angles = jnp.arange(tensor.shape[-2], dtype=jnp.float32)[:, None] * frequency[None, :]
    cosine = jnp.cos(angles)
    sine_part = direction * jnp.sin(angles)
    lower_part = tensor[..., :middle].astype(jnp.float32)
    upper_part = tensor[..., middle:].astype(jnp.float32)
    return jnp.concatenate([lower_part * cosine - upper_part * sine_part, lower_part * sine_part + upper_part * cosine], axis=-1)

def to_bfloat(tensor):
    return lax.optimization_barrier(tensor.astype(jnp.bfloat16)).astype(jnp.float32)

def live_scores(query_rows, key_rows, key_counts):
    scaling = 1.0 / math.sqrt(query_rows.shape[-1])
    scores = jnp.einsum('zhid,zhjd->zhij', query_rows.astype(jnp.float32), key_rows.astype(jnp.float32)) * scaling
    usable = jnp.arange(key_rows.shape[-2])[None, None, None, :] < key_counts[:, None, None, None]
    return jnp.where(usable, scores, -jnp.inf)

def neighbour_forward(query_rows, key_rows, value_rows, key_counts):
    scores = live_scores(query_rows, key_rows, key_counts)
    maxima = lax.optimization_barrier(jnp.max(scores, axis=-1, keepdims=True))
    weights = jnp.exp(scores - maxima)
    totals = lax.optimization_barrier(jnp.sum(weights, axis=-1))
    summed = jnp.einsum('zhij,zhjd->zhid', to_bfloat(weights), value_rows.astype(jnp.float32))
    return (summed / totals[..., None], maxima[..., 0] + jnp.log(totals))

def neighbour_backward(query_rows, key_rows, value_rows, key_counts, grad_rows, log_totals, output_dots):
    scaling = 1.0 / math.sqrt(query_rows.shape[-1])
    scores = live_scores(query_rows, key_rows, key_counts)
    chances = jnp.exp(scores - log_totals[..., None])
    grad_values = jnp.einsum('zhij,zhid->zhjd', to_bfloat(chances), grad_rows.astype(jnp.float32))
    grad_weights = jnp.einsum('zhid,zhjd->zhij', grad_rows.astype(jnp.float32), value_rows.astype(jnp.float32))
    grad_scores = to_bfloat(chances * (grad_weights - output_dots[..., None]) * scaling)
    grad_query = to_bfloat(jnp.einsum('zhij,zhjd->zhid', grad_scores, key_rows.astype(jnp.float32)))
    grad_key = jnp.einsum('zhij,zhid->zhjd', grad_scores, query_rows.astype(jnp.float32))
    return (grad_query, grad_key, grad_values)

def reference(queries, keys, values, cotangent, lengths):
    rim_rows = SPAN - 1
    row_width = HEADS * DH

    def windows(tokens):
        padded = jnp.concatenate([tokens[:, rim_rows:], jnp.zeros((BATCH, rim_rows, row_width), tokens.dtype)], axis=1)
        return padded.reshape(BATCH * SPANS, SPAN, HEADS, DH).transpose(0, 2, 1, 3)
    query_windows = rotate(windows(queries), 1.0).astype(jnp.bfloat16)
    grad_windows = windows(cotangent)
    key_turned = rotate(keys.reshape(BATCH * SPANS, NBR, HEADS, NEIGH, DH), 1.0).astype(jnp.bfloat16)
    value_rows = values.reshape(BATCH * SPANS, NBR, HEADS, NEIGH, DH)
    key_counts = lengths.reshape(BATCH * SPANS, NBR).astype(jnp.int32)

    def span_work(pieces):
        query_one, grad_one, key_one, value_one, counts_one = pieces
        query_pair = jnp.broadcast_to(query_one[None], (NBR,) + query_one.shape)
        grad_pair = jnp.broadcast_to(grad_one[None], (NBR,) + grad_one.shape)
        partial_value, log_parts = neighbour_forward(query_pair, key_one, value_one, counts_one)
        log_whole = jax.nn.logsumexp(log_parts, axis=0)
        attended = lax.optimization_barrier(jnp.sum(jnp.exp(log_parts - log_whole[None])[..., None] * partial_value, axis=0)).astype(jnp.bfloat16)
        output_dots = lax.optimization_barrier(jnp.sum(grad_one.astype(jnp.float32) * attended.astype(jnp.float32), axis=-1))
        grad_query, grad_key, grad_values = neighbour_backward(query_pair, key_one, value_one, counts_one, grad_pair, jnp.broadcast_to(log_whole[None], log_parts.shape), jnp.broadcast_to(output_dots[None], log_parts.shape))
        return (attended, lax.optimization_barrier(jnp.sum(grad_query, axis=0)), grad_key, grad_values.astype(jnp.bfloat16))
    attended, grad_sum, grad_key, grad_values = lax.map(span_work, (query_windows, grad_windows, key_turned, value_rows, key_counts))

    def tokens_of(window_rows):
        flat_rows = window_rows.transpose(0, 2, 1, 3).reshape(BATCH, SEQ, row_width)
        return jnp.concatenate([jnp.zeros((BATCH, rim_rows, row_width), flat_rows.dtype), flat_rows[:, :SEQ - rim_rows]], axis=1)
    grad_windows_out = rotate(grad_sum, -1.0).astype(jnp.bfloat16)
    grad_keys = rotate(grad_key, -1.0).astype(jnp.bfloat16).reshape(keys.shape)
    return (tokens_of(attended), tokens_of(grad_windows_out), grad_keys, grad_values.reshape(values.shape))
```

```python
import functools
import math

import jax
import jax.numpy as jnp
import numpy as np
from jax import lax
from jax.experimental import pallas as pl
from jax.experimental.pallas import tpu as pltpu
from jax.sharding import PartitionSpec as P

DH = 128
SPAN = 64
NBR = 2
NEIGH = 128
N_Z = 16
N_CTX = 32
N_TP = 4
HEADS_HERE = 8
SCALE = 1.0 / math.sqrt(DH)
BF = jnp.bfloat16
F32 = jnp.float32
VMEM = pl.BlockSpec(memory_space=pltpu.VMEM)
SMEM = pl.BlockSpec(memory_space=pltpu.SMEM)
LIMIT = 40 * 1024 * 1024


def flat(ctx, tp):
    return ctx * N_TP + tp


def worker(ctx, t1, span):
    return flat(N_Z * t1 + ctx % N_Z, 2 * span + ((ctx // N_Z) ^ t1))


def routes():
    big, tiny = [], []
    for k in range(2):
        big.append([(flat(c, t), worker(c, t // 2, (t % 2) ^ k)) for c in range(N_CTX) for t in range(N_TP)])
        tiny.append([(flat(c, 2 * t1 + k), worker((c + 1) % N_CTX, t1, 1)) for c in range(N_CTX) for t1 in range(2)])
    return big, tiny


def turned_round(pairs):
    return [(b, a) for a, b in pairs]


def z_groups():
    groups = []
    for y in range(2):
        for t in range(N_TP):
            groups.append([flat(N_Z * y + (j ^ (8 * (t // 2))), t) for j in range(N_Z)])
    return groups


def tables(indices):
    freq = 10000.0 ** (-2.0 * np.arange(DH // 2, dtype=np.float64) / DH)
    angles = np.asarray(indices, np.float64)[:, None] * freq[None]
    cos, sin = np.cos(angles), np.sin(angles)
    return (
        np.concatenate([cos, cos], 1).astype(np.float32),
        np.concatenate([-sin, sin], 1).astype(np.float32),
    )


def half_turn(x):
    return pltpu.roll(x, DH // 2, 1)


def dot(a, b, da, db):
    return lax.dot_general(a, b, (((da,), (db,)), ((), ())), preferred_element_type=F32)


def block_of(span, y_half, slot):
    return lax.rem(N_Z * y_half + lax.bitwise_xor(slot, 8 * span) - span + N_CTX, N_CTX)


def pack_kernel(meta, q_ref, g_ref, r0_ref, r1_ref, t_ref):
    t0, ctx = meta[3], meta[4]
    last = lax.broadcasted_iota(jnp.int32, (SPAN, DH), 0) == SPAN - 1
    edges = []
    for h in range(HEADS_HERE):
        for a, ref in enumerate((q_ref, g_ref)):
            low = ref[0:SPAN, h * DH : (h + 1) * DH].astype(F32)
            high = ref[SPAN : 2 * SPAN, h * DH : (h + 1) * DH].astype(F32)
            edges.append(high[SPAN - 1 :])
            even = jnp.where(last, low[SPAN - 1 :], high).astype(BF)
            odd = jnp.where(ctx == 0, 0.0, low).astype(BF)

            @pl.when(t0 == 0)
            def _():
                r0_ref[h, a] = even
                r1_ref[h, a] = odd

            @pl.when(t0 != 0)
            def _():
                r0_ref[h, a] = odd
                r1_ref[h, a] = even

    t_ref[...] = jnp.concatenate(edges, axis=0).astype(BF)


def join_kernel(meta, r0_ref, r1_ref, t0_ref, t1_ref, out_ref):
    odd = meta[0] == 1
    last = jnp.logical_and(lax.broadcasted_iota(jnp.int32, (SPAN, DH), 0) == SPAN - 1, odd)
    for k, (r_ref, t_ref) in enumerate(((r0_ref, t1_ref), (r1_ref, t0_ref))):
        edge = t_ref[...].astype(F32)
        for h in range(HEADS_HERE):
            for a in range(2):
                row = edge[2 * h + a : 2 * h + a + 1]
                out_ref[8 * k + h, a] = jnp.where(last, row, r_ref[h, a].astype(F32)).astype(BF)


def prep_kernel(meta, k_ref, v_ref, cos_ref, sin_ref, kl_ref, vl_ref, send_ref):
    cos, sin = cos_ref[...], sin_ref[...]

    def turn(x):
        x = x.astype(F32)
        return (x * cos + half_turn(x) * sin).astype(BF)

    def step(j, carry):
        mine = block_of(meta[0], meta[1], j)
        theirs = block_of(meta[0], 1 - meta[1], j)
        kl_ref[j] = turn(k_ref[mine])
        vl_ref[j] = v_ref[mine]
        send_ref[0, j] = turn(k_ref[theirs])
        send_ref[1, j] = v_ref[theirs]
        return carry

    lax.fori_loop(0, N_Z, step, 0)


GROUP = 4


def main_kernel(
    meta, len_ref, x_ref, kl_ref, vl_ref, o_ref, qc_ref, qs_ref, kc_ref, ks_ref,
    out_ref, dk_ref, dv_ref, send_ref,
):
    span, y_half, nbr = meta[0], meta[1], meta[2]
    base = pl.program_id(0) * GROUP
    qc, qs = qc_ref[...], qs_ref[...]
    kc, ks = kc_ref[...], ks_ref[...]
    lane = lax.broadcasted_iota(jnp.int32, (SPAN, NEIGH), 1)
    for w in range(GROUP):
        unit = 2 * block_of(span, y_half, base + w) + span
        lens = (len_ref[NBR * unit + nbr], len_ref[NBR * unit + 1 - nbr])
        keys = (kl_ref[w], o_ref[0, w])
        vals = (vl_ref[w], o_ref[1, w])
        q = x_ref[w, 0].astype(F32)
        qw = (q * qc + half_turn(q) * qs).astype(BF)
        g = x_ref[w, 1]
        es, ms, ts, os = [], [], [], []
        for n in range(NBR):
            s = jnp.where(lane < lens[n], dot(qw, keys[n], 1, 1) * SCALE, -jnp.inf)
            m = jnp.max(s, axis=1, keepdims=True)
            e = jnp.exp(s - m)
            es.append(e)
            ms.append(m)
            ts.append(jnp.sum(e, axis=1, keepdims=True))
            os.append(dot(e.astype(BF), vals[n], 1, 0))
        top = jnp.maximum(ms[0], ms[1])
        parts = [jnp.exp(m - top) for m in ms]
        inv = 1.0 / (parts[0] * ts[0] + parts[1] * ts[1])
        ws = [p * inv for p in parts]
        att = (ws[0] * os[0] + ws[1] * os[1]).astype(BF)
        out_ref[w, 0] = att
        dots = jnp.sum(g.astype(F32) * att.astype(F32), axis=1, keepdims=True)
        gq = jnp.zeros((SPAN, DH), F32)
        for n in range(NBR):
            pr = es[n] * ws[n]
            gw = dot(g, vals[n], 1, 1)
            gs = (pr * (gw - dots) * SCALE).astype(BF)
            gq = gq + dot(gs, keys[n], 1, 0).astype(BF).astype(F32)
            dk = dot(gs, qw, 0, 0)
            dk = (dk * kc - half_turn(dk) * ks).astype(BF)
            dv = dot(pr.astype(BF), g, 0, 0).astype(BF)
            if n == 0:
                dk_ref[w] = dk
                dv_ref[w] = dv
            else:
                send_ref[0, w] = dk
                send_ref[1, w] = dv
        out_ref[w, 1] = (gq * qc - half_turn(gq) * qs).astype(BF)


def settle_kernel(meta, dk_ref, dv_ref, got_ref, gk_ref, gv_ref):
    def step(j, carry):
        mine = block_of(meta[0], meta[1], j)
        theirs = block_of(meta[0], 1 - meta[1], j)
        gk_ref[mine] = dk_ref[j]
        gv_ref[mine] = dv_ref[j]
        gk_ref[theirs] = got_ref[0, j]
        gv_ref[theirs] = got_ref[1, j]
        return carry

    lax.fori_loop(0, N_Z, step, 0)


def unpack_kernel(meta, r0_ref, r1_ref, t0_ref, t1_ref, att_ref, gq_ref):
    t0, ctx = meta[3], meta[4]
    last = lax.broadcasted_iota(jnp.int32, (SPAN, DH), 0) == SPAN - 1
    edge = jnp.where(t0 == 0, t1_ref[...].astype(F32), t0_ref[...].astype(F32))
    for h in range(HEADS_HERE):
        for a, ref in enumerate((att_ref, gq_ref)):
            one = r0_ref[h, a].astype(F32)
            two = r1_ref[h, a].astype(F32)
            even = jnp.where(t0 == 0, one, two)
            odd = jnp.where(t0 == 0, two, one)
            odd = jnp.where(ctx == 0, 0.0, odd)
            row = edge[2 * h + a : 2 * h + a + 1]
            ref[0:SPAN, h * DH : (h + 1) * DH] = jnp.where(last, even[SPAN - 1 :], odd).astype(BF)
            ref[SPAN : 2 * SPAN, h * DH : (h + 1) * DH] = jnp.where(last, row, even).astype(BF)


def shaped(*shape):
    return jax.ShapeDtypeStruct(shape, BF)


def call(kernel, outs, n_vmem, flops=1000, moved=1000, **more):
    return pl.pallas_call(
        kernel,
        out_shape=outs,
        in_specs=[SMEM] + [VMEM] * n_vmem,
        out_specs=jax.tree.map(lambda _: VMEM, outs),
        compiler_params=pltpu.CompilerParams(vmem_limit_bytes=LIMIT),
        cost_estimate=pl.CostEstimate(flops=flops, bytes_accessed=moved, transcendentals=0),
        **more,
    )


def shards(queries, keys, values, cotangent, lengths):
    both = ("ctx", "tp")
    ctx, tp = lax.axis_index("ctx"), lax.axis_index("tp")
    span, nbr = tp // 2, tp % 2
    meta = jnp.stack([span, (ctx // N_Z) ^ nbr, nbr, tp % 2, ctx]).astype(jnp.int32)
    big, tiny = routes()
    chunk = shaped(HEADS_HERE, 2, SPAN, DH)
    edge = shaped(2 * HEADS_HERE, DH)
    qc, qs = map(jnp.asarray, tables([*range(1, SPAN), 0]))
    kc, ks = map(jnp.asarray, tables(range(NEIGH)))

    r0, r1, t = call(pack_kernel, (chunk, chunk, edge), 2, moved=1 << 20)(meta, queries[0], cotangent[0])
    r0 = lax.ppermute(r0, both, big[0])
    r1 = lax.ppermute(r1, both, big[1])
    e0 = lax.ppermute(t, both, tiny[0])
    e1 = lax.ppermute(t, both, tiny[1])

    half = shaped(N_Z, NEIGH, DH)
    pair = shaped(2, N_Z, NEIGH, DH)
    k_mine, v_mine, kv_send = call(prep_kernel, (half, half, pair), 4, flops=1 << 24, moved=4 << 20)(
        meta, keys.reshape(N_CTX, NEIGH, DH), values.reshape(N_CTX, NEIGH, DH), kc, ks
    )
    joined = call(join_kernel, shaped(2 * HEADS_HERE, 2, SPAN, DH), 4, moved=1 << 20)(meta, r0, r1, e0, e1)
    kv_send, joined = lax.optimization_barrier((kv_send, joined))
    swap = [(i, i ^ 1) for i in range(N_TP)]
    kv_got = lax.ppermute(kv_send, "tp", swap)
    rows = lax.all_to_all(joined, both, 0, 0, axis_index_groups=z_groups(), tiled=True)

    steps = N_Z // GROUP
    by_slot = lambda *tail: pl.BlockSpec((GROUP,) + tail, lambda i, *_: (i,) + (0,) * len(tail))
    paired = pl.BlockSpec((2, GROUP, NEIGH, DH), lambda i, *_: (0, i, 0, 0))
    whole = lambda n: pl.BlockSpec((n, DH), lambda i, *_: (0, 0))
    out, dk, dv, d_send = pl.pallas_call(
        main_kernel,
        out_shape=(shaped(N_Z, 2, SPAN, DH), half, half, pair),
        grid_spec=pltpu.PrefetchScalarGridSpec(
            num_scalar_prefetch=2,
            grid=(steps,),
            in_specs=[
                by_slot(2, SPAN, DH), by_slot(NEIGH, DH), by_slot(NEIGH, DH), paired,
                whole(SPAN), whole(SPAN), whole(NEIGH), whole(NEIGH),
            ],
            out_specs=[by_slot(2, SPAN, DH), by_slot(NEIGH, DH), by_slot(NEIGH, DH), paired],
        ),
        compiler_params=pltpu.CompilerParams(vmem_limit_bytes=LIMIT),
        cost_estimate=pl.CostEstimate(flops=1 << 29, bytes_accessed=6 << 20, transcendentals=1 << 18),
    )(meta, lengths.reshape(-1), rows, k_mine, v_mine, kv_got, qc, qs, kc, ks)

    d_got = lax.ppermute(d_send, "tp", swap)
    back = lax.all_to_all(out, both, 0, 0, axis_index_groups=z_groups(), tiled=True)
    full = shaped(N_CTX, NEIGH, DH)
    gk, gv = call(settle_kernel, (full, full), 3, moved=4 << 20)(meta, dk, dv, d_got)

    r0 = lax.ppermute(back[:HEADS_HERE], both, turned_round(big[0]))
    r1 = lax.ppermute(back[HEADS_HERE:], both, turned_round(big[1]))
    rims = back[:, :, SPAN - 1, :].reshape(2, 2 * HEADS_HERE, DH)
    e1 = lax.ppermute(rims[0], both, turned_round(tiny[1]))
    e0 = lax.ppermute(rims[1], both, turned_round(tiny[0]))
    wide = shaped(2 * SPAN, HEADS_HERE * DH)
    att, gq = call(unpack_kernel, (wide, wide), 4, moved=1 << 20)(meta, r0, r1, e1, e0)
    return att[None], gq[None], gk.reshape(keys.shape), gv.reshape(values.shape)


def solution(mesh):
    in_specs = (
        P("dp", "ctx", "tp"),
        P("dp", None, "tp", "ctx", None, None),
        P("dp", None, "tp", "ctx", None, None),
        P("dp", "ctx", "tp"),
        P("dp", None, None),
    )
    out_specs = (
        P("dp", "ctx", "tp"),
        P("dp", "ctx", "tp"),
        P("dp", None, "tp", "ctx", None, None),
        P("dp", None, "tp", "ctx", None, None),
    )
    return jax.shard_map(shards, mesh=mesh, in_specs=in_specs, out_specs=out_specs, check_vma=False)
```

```python
import functools
import math

import jax
import jax.numpy as jnp
import numpy as np
from jax import lax
from jax.experimental import pallas as pl
from jax.experimental.pallas import tpu as pltpu
from jax.sharding import PartitionSpec as P

DH = 128
SPAN = 64
NBR = 2
NEIGH = 128
N_Z = 16
N_CTX = 32
N_TP = 4
HEADS_HERE = 8
WINDOWS = N_Z + 1
GROUP = 6
SLOTS = 18
SCALE = 1.0 / math.sqrt(DH)
BF = jnp.bfloat16
F32 = jnp.float32
VMEM = pl.BlockSpec(memory_space=pltpu.VMEM)
SMEM = pl.BlockSpec(memory_space=pltpu.SMEM)
HBM = pl.BlockSpec(memory_space=pltpu.HBM)
LIMIT = 12 * 1024 * 1024
TURN_COST = 11 << 30
TURN_BYTES = 2 << 20


def flat(ctx, tp):
    return ctx * N_TP + tp


def worker(ctx, t1, span):
    return flat(N_Z * t1 + ctx % N_Z, 2 * span + ((ctx // N_Z) ^ t1))


def routes():
    return [
        [(flat(c, t), worker(c, t // 2, (t % 2) ^ k)) for c in range(N_CTX) for t in range(N_TP)]
        for k in range(2)
    ]


def turned_round(pairs):
    return [(b, a) for a, b in pairs]


def z_groups():
    groups = []
    for y in range(2):
        for t in range(N_TP):
            groups.append([flat(N_Z * y + (j ^ (8 * (t // 2))), t) for j in range(N_Z)])
    return groups


def tables(indices):
    freq = 10000.0 ** (-2.0 * np.arange(DH // 2, dtype=np.float64) / DH)
    angles = np.asarray(indices, np.float64)[:, None] * freq[None]
    cos, sin = np.cos(angles), np.sin(angles)
    return (
        np.concatenate([cos, cos], 1).astype(np.float32),
        np.concatenate([-sin, sin], 1).astype(np.float32),
    )


def half_turn(x):
    return pltpu.roll(x, DH // 2, 1)


def dot(a, b, da, db):
    return lax.dot_general(a, b, (((da,), (db,)), ((), ())), preferred_element_type=F32)


def block_of(span, y_half, w):
    return jnp.clip(N_Z * y_half - span + w, 0, N_CTX - 1)


def place(z, span):
    return lax.bitwise_xor(z, 8 * span)


def is_last():
    return lax.broadcasted_iota(jnp.int32, (SPAN, DH), 0) == SPAN - 1


def pack_kernel(meta, q_ref, g_ref, r0_ref, r1_ref):
    t0, ctx = meta[3], meta[4]
    last = is_last()
    gone = jnp.logical_and(ctx == 0, jnp.logical_not(last))
    for h in range(HEADS_HERE):
        for a, ref in enumerate((q_ref, g_ref)):
            low = ref[0:SPAN, h * DH : (h + 1) * DH].astype(F32)
            high = ref[SPAN : 2 * SPAN, h * DH : (h + 1) * DH].astype(F32)
            even = jnp.where(last, low, high)
            odd = jnp.where(gone, 0.0, jnp.where(last, high, low))
            r0_ref[h, a] = jnp.where(t0 == 0, even, odd).astype(BF)
            r1_ref[h, a] = jnp.where(t0 == 0, odd, even).astype(BF)


def first_of(span, y_half):
    return jnp.clip(N_Z * y_half - span, 0, N_Z - 1)


def send_kernel(meta, k_ref, v_ref, out_ref, sem):
    blocks = pl.ds(first_of(meta[0], 1 - meta[1]), WINDOWS)
    copies = [pltpu.make_async_copy(ref.at[blocks], out_ref.at[n], sem.at[n]) for n, ref in enumerate((k_ref, v_ref))]
    for copy in copies:
        copy.start()
    for copy in copies:
        copy.wait()


def turn_kernel(meta, k_ref, v_ref, got_ref, cos_ref, sin_ref, out_ref):
    cos, sin = cos_ref[...], sin_ref[...]

    def turn(x):
        x = x.astype(F32)
        return (x * cos + half_turn(x) * sin).astype(BF)

    def step(w, carry):
        block = block_of(meta[0], meta[1], w)
        far = block - first_of(meta[0], meta[1])
        out_ref[w, 0] = turn(k_ref[block])
        out_ref[w, 1] = turn(got_ref[0, far])
        out_ref[w, 2] = v_ref[block]
        out_ref[w, 3] = got_ref[1, far]
        return carry

    lax.fori_loop(0, WINDOWS, step, 0)


def main_kernel(
    meta, len_ref, x_ref, kv_ref, qc_ref, qs_ref, kc_ref, ks_ref,
    out_hbm, local_hbm, send_hbm, out_ref, local_ref, send_ref, done_ref, out_sem, grad_sem,
):
    span, y_half, nbr = meta[0], meta[1], meta[2]
    qc, qs = qc_ref[...], qs_ref[...]
    kc, ks = kc_ref[...], ks_ref[...]
    lane = lax.broadcasted_iota(jnp.int32, (SPAN, NEIGH), 1)
    last = is_last()
    these = range(GROUP)
    each = [(i, n) for i in these for n in range(NBR)]

    def group(step, carry):
        places = [step * GROUP + i for i in these]
        slots = [jnp.minimum(w, WINDOWS - 1) for w in places]
        blocks = [block_of(span, y_half, w) for w in slots]

        def rows(w, a):
            body = jnp.where(w < N_Z, x_ref[place(jnp.minimum(w, N_Z - 1), span), a].astype(F32), 0.0)
            v = w - span
            edge = jnp.logical_and(v >= 0, v < N_Z)
            edge = jnp.where(edge, x_ref[place(jnp.clip(v, 0, N_Z - 1), span), a].astype(F32), 0.0)
            return jnp.where(last, edge, body)

        def live(i, n):
            unit = NBR * (2 * blocks[i] + span)
            return lane < len_ref[unit + (nbr if n == 0 else 1 - nbr)]

        keys = {(i, n): kv_ref[slots[i], n] for i, n in each}
        vals = {(i, n): kv_ref[slots[i], 2 + n] for i, n in each}
        q = [rows(w, 0) for w in places]
        gf = [rows(w, 1) for w in places]
        qw = [(x * qc + half_turn(x) * qs).astype(BF) for x in q]
        g = [x.astype(BF) for x in gf]
        s = {k: dot(qw[k[0]], keys[k], 1, 1) for k in each}
        gv = {k: dot(g[k[0]], vals[k], 1, 1) for k in each}
        s = {k: jnp.where(live(*k), s[k] * SCALE, -jnp.inf) for k in each}
        m = {k: jnp.max(s[k], axis=1, keepdims=True) for k in each}
        e = {k: jnp.exp(s[k] - m[k]) for k in each}
        total = {k: jnp.sum(e[k], axis=1, keepdims=True) for k in each}
        o = {k: dot(e[k].astype(BF), vals[k], 1, 0) for k in each}
        top = [jnp.maximum(m[i, 0], m[i, 1]) for i in these]
        part = {k: jnp.exp(m[k] - top[k[0]]) for k in each}
        inv = [1.0 / (part[i, 0] * total[i, 0] + part[i, 1] * total[i, 1]) for i in these]
        share = {k: part[k] * inv[k[0]] for k in each}
        att = [(share[i, 0] * o[i, 0] + share[i, 1] * o[i, 1]).astype(BF) for i in these]
        dots = [jnp.sum(gf[i] * att[i].astype(F32), axis=1, keepdims=True) for i in these]
        pr = {k: e[k] * share[k] for k in each}
        gs = {k: (pr[k] * (gv[k] - dots[k[0]]) * SCALE).astype(BF) for k in each}
        gq = {k: dot(gs[k], keys[k], 1, 0).astype(BF).astype(F32) for k in each}
        gq = [gq[i, 0] + gq[i, 1] for i in these]
        dk = {k: dot(gs[k], qw[k[0]], 0, 0) for k in each}
        dv = {k: dot(pr[k].astype(BF), g[k[0]], 0, 0).astype(BF) for k in each}
        dk = {k: (dk[k] * kc - half_turn(dk[k]) * ks).astype(BF) for k in each}
        for i, w in enumerate(places):
            done_ref[w, 0] = att[i]
            done_ref[w, 1] = (gq[i] * qc - half_turn(gq[i]) * qs).astype(BF)
            local_ref[w, 0] = dk[i, 0]
            local_ref[w, 1] = dv[i, 0]
            send_ref[w, 0] = dk[i, 1]
            send_ref[w, 1] = dv[i, 1]
        for copy in grads(step):
            copy.start()

        def whole(z, carry):
            for a in range(2):
                mine, edge = done_ref[z, a].astype(F32), done_ref[z + span, a].astype(F32)
                out_ref[z, a] = jnp.where(last, edge, mine).astype(BF)
            rows_out(z).start()
            return carry

        end = jnp.minimum(GROUP * (step + 1) - 1, N_Z)
        lax.fori_loop(jnp.maximum(GROUP * step - 1, 0), end, whole, 0)
        return carry

    def grads(step):
        these_slots = pl.ds(step * GROUP, GROUP)
        return [
            pltpu.make_async_copy(ref.at[these_slots], hbm.at[these_slots], grad_sem.at[step, n])
            for n, (ref, hbm) in enumerate(((local_ref, local_hbm), (send_ref, send_hbm)))
        ]

    def rows_out(z):
        return pltpu.make_async_copy(out_ref.at[z], out_hbm.at[place(z, span)], out_sem.at[z])

    lax.fori_loop(0, SLOTS // GROUP, group, 0)

    def finish(step, carry):
        for copy in grads(step):
            copy.wait()
        return carry

    lax.fori_loop(0, SLOTS // GROUP, finish, 0)

    def finish_rows(z, carry):
        rows_out(z).wait()
        return carry

    lax.fori_loop(0, N_Z, finish_rows, 0)


def settle_kernel(meta, local_ref, got_ref, gk_ref, gv_ref):
    span, y_half = meta[0], meta[1]

    def step(i, carry):
        mine, theirs = N_Z * y_half + i, N_Z * (1 - y_half) + i
        for n, ref in enumerate((gk_ref, gv_ref)):
            ref[mine] = local_ref[i + span, n]
            ref[theirs] = got_ref[i + span, n]
        return carry

    lax.fori_loop(0, N_Z, step, 0, unroll=4)

    @pl.when(span == 1)
    def _():
        mine, theirs = jnp.where(y_half == 0, N_Z, 0), jnp.where(y_half == 0, 0, N_Z)
        for n, ref in enumerate((gk_ref, gv_ref)):
            ref[N_Z - 1] = (local_ref[mine, n].astype(F32) + got_ref[theirs, n].astype(F32)).astype(BF)


def unpack_kernel(meta, r0_ref, r1_ref, att_ref, gq_ref):
    t0, ctx = meta[3], meta[4]
    last = is_last()
    gone = jnp.logical_and(ctx == 0, jnp.logical_not(last))
    for h in range(HEADS_HERE):
        for a, ref in enumerate((att_ref, gq_ref)):
            one = r0_ref[h, a].astype(F32)
            two = r1_ref[h, a].astype(F32)
            even = jnp.where(t0 == 0, one, two)
            odd = jnp.where(gone, 0.0, jnp.where(t0 == 0, two, one))
            ref[0:SPAN, h * DH : (h + 1) * DH] = jnp.where(last, even, odd).astype(BF)
            ref[SPAN : 2 * SPAN, h * DH : (h + 1) * DH] = jnp.where(last, odd, even).astype(BF)


def shaped(*shape):
    return jax.ShapeDtypeStruct(shape, BF)


def in_hbm(*shape):
    return pltpu.HBM(shape, BF)


def call(kernel, outs, n_vmem, flops=1000, moved=1000, **more):
    return pl.pallas_call(
        kernel,
        out_shape=outs,
        in_specs=[SMEM] + [VMEM] * n_vmem,
        out_specs=jax.tree.map(lambda _: VMEM, outs),
        compiler_params=pltpu.CompilerParams(vmem_limit_bytes=LIMIT),
        cost_estimate=pl.CostEstimate(flops=flops, bytes_accessed=moved, transcendentals=0),
        **more,
    )


def shards(queries, keys, values, cotangent, lengths):
    both = ("ctx", "tp")
    ctx, tp = lax.axis_index("ctx"), lax.axis_index("tp")
    span, nbr = tp // 2, tp % 2
    meta = jnp.stack([span, (ctx // N_Z) ^ nbr, nbr, tp % 2, ctx]).astype(jnp.int32)
    routes_out = routes()
    chunk = shaped(HEADS_HERE, 2, SPAN, DH)
    qc, qs = map(jnp.asarray, tables([*range(1, SPAN), 0]))
    kc, ks = map(jnp.asarray, tables(range(NEIGH)))
    swap = [(i, i ^ 1) for i in range(N_TP)]

    r0, r1 = call(pack_kernel, (chunk, chunk), 2, moved=1 << 20)(meta, queries[0], cotangent[0])
    r0, r1, meta_then = lax.optimization_barrier((r0, r1, meta))
    r0 = lax.ppermute(r0, both, routes_out[0])
    r1 = lax.ppermute(r1, both, routes_out[1])

    pair = shaped(2, WINDOWS, NEIGH, DH)
    keys_here, values_here = keys.reshape(N_CTX, NEIGH, DH), values.reshape(N_CTX, NEIGH, DH)
    kv_send = pl.pallas_call(
        send_kernel,
        out_shape=pair,
        in_specs=[SMEM, HBM, HBM],
        out_specs=VMEM,
        scratch_shapes=[pltpu.SemaphoreType.DMA((2,))],
        compiler_params=pltpu.CompilerParams(vmem_limit_bytes=LIMIT),
        cost_estimate=pl.CostEstimate(flops=0, bytes_accessed=2 << 20, transcendentals=0),
    )(meta_then, *(pltpu.with_memory_space_constraint(x, pltpu.HBM) for x in (keys_here, values_here)))
    kv_got = lax.ppermute(kv_send, "tp", swap)
    turned = call(turn_kernel, shaped(WINDOWS, 4, NEIGH, DH), 5, flops=TURN_COST, moved=TURN_BYTES)(
        meta, keys_here, values_here, kv_got, kc, ks
    )
    joined = jnp.concatenate([r0, r1], axis=0)
    rows = lax.all_to_all(joined, both, 0, 0, axis_index_groups=z_groups(), tiled=True)

    grads = shaped(SLOTS, 2, NEIGH, DH)
    row_set = (N_Z, 2, SPAN, DH)
    out, d_local, d_send = pl.pallas_call(
        main_kernel,
        out_shape=(in_hbm(*row_set), in_hbm(*grads.shape), in_hbm(*grads.shape)),
        in_specs=[SMEM, SMEM] + [VMEM] * 6,
        out_specs=(HBM,) * 3,
        scratch_shapes=[
            pltpu.VMEM(row_set, BF),
            pltpu.VMEM(grads.shape, BF),
            pltpu.VMEM(grads.shape, BF),
            pltpu.VMEM((SLOTS, 2, SPAN, DH), BF),
            pltpu.SemaphoreType.DMA((N_Z,)),
            pltpu.SemaphoreType.DMA((SLOTS // GROUP, 2)),
        ],
        compiler_params=pltpu.CompilerParams(vmem_limit_bytes=LIMIT),
        cost_estimate=pl.CostEstimate(flops=1 << 29, bytes_accessed=6 << 20, transcendentals=1 << 18),
    )(meta, lengths.reshape(-1), rows, turned, qc, qs, kc, ks)

    back = lax.all_to_all(out, both, 0, 0, axis_index_groups=z_groups(), tiled=True)
    d_got = lax.ppermute(d_send, "tp", swap)
    full = shaped(N_CTX, NEIGH, DH)
    gk, gv = call(settle_kernel, (full, full), 2, moved=4 << 20)(meta, d_local, d_got)

    r0 = lax.ppermute(back[:HEADS_HERE], both, turned_round(routes_out[0]))
    r1 = lax.ppermute(back[HEADS_HERE:], both, turned_round(routes_out[1]))
    wide = shaped(2 * SPAN, HEADS_HERE * DH)
    att, gq = call(unpack_kernel, (wide, wide), 2, moved=1 << 20)(meta, r0, r1)
    return att[None], gq[None], gk.reshape(keys.shape), gv.reshape(values.shape)


def solution(mesh):
    in_specs = (
        P("dp", "ctx", "tp"),
        P("dp", None, "tp", "ctx", None, None),
        P("dp", None, "tp", "ctx", None, None),
        P("dp", "ctx", "tp"),
        P("dp", None, None),
    )
    out_specs = (
        P("dp", "ctx", "tp"),
        P("dp", "ctx", "tp"),
        P("dp", None, "tp", "ctx", None, None),
        P("dp", None, "tp", "ctx", None, None),
    )
    return jax.shard_map(shards, mesh=mesh, in_specs=in_specs, out_specs=out_specs, check_vma=False)
```

```python
import functools
import math

import jax
import jax.numpy as jnp
import numpy as np
from jax import lax
from jax.experimental import pallas as pl
from jax.experimental.pallas import tpu as pltpu
from jax.sharding import PartitionSpec as P

DH = 128
SPAN = 64
NBR = 2
NEIGH = 128
N_Z = 16
N_CTX = 32
N_TP = 4
N_DP = 4
HEADS_HERE = 8
WINDOWS = N_Z + 1
GROUP = 6
SLOTS = 18
SCALE = 1.0 / math.sqrt(DH)
BF = jnp.bfloat16
F32 = jnp.float32
VMEM = pl.BlockSpec(memory_space=pltpu.VMEM)
SMEM = pl.BlockSpec(memory_space=pltpu.SMEM)
HBM = pl.BlockSpec(memory_space=pltpu.HBM)
LIMIT = 12 * 1024 * 1024
TURN_COST = 11 << 30
TURN_BYTES = 2 << 20


def flat(ctx, tp):
    return ctx * N_TP + tp


def worker(ctx, t1, span):
    return flat(N_Z * t1 + ctx % N_Z, 2 * span + ((ctx // N_Z) ^ t1))


def routes():
    return [
        [(flat(c, t), worker(c, t // 2, (t % 2) ^ k)) for c in range(N_CTX) for t in range(N_TP)]
        for k in range(2)
    ]


def turned_round(pairs):
    return [(b, a) for a, b in pairs]


def z_groups():
    groups = []
    for y in range(2):
        for t in range(N_TP):
            groups.append([flat(N_Z * y + (j ^ (8 * (t // 2))), t) for j in range(N_Z)])
    return groups


def tables(indices):
    freq = 10000.0 ** (-2.0 * np.arange(DH // 2, dtype=np.float64) / DH)
    angles = np.asarray(indices, np.float64)[:, None] * freq[None]
    cos, sin = np.cos(angles), np.sin(angles)
    return (
        np.concatenate([cos, cos], 1).astype(np.float32),
        np.concatenate([-sin, sin], 1).astype(np.float32),
    )


def half_turn(x):
    return pltpu.roll(x, DH // 2, 1)


def dot(a, b, da, db):
    return lax.dot_general(a, b, (((da,), (db,)), ((), ())), preferred_element_type=F32)


def block_of(span, y_half, w):
    return jnp.clip(N_Z * y_half - span + w, 0, N_CTX - 1)


def place(z, span):
    return lax.bitwise_xor(z, 8 * span)


def is_last():
    return lax.broadcasted_iota(jnp.int32, (SPAN, DH), 0) == SPAN - 1


def pack_kernel(meta, q_ref, g_ref, r0_ref, r1_ref):
    t0, ctx = meta[3], meta[4]
    last = is_last()
    gone = jnp.logical_and(ctx == 0, jnp.logical_not(last))
    for h in range(HEADS_HERE):
        for a, ref in enumerate((q_ref, g_ref)):
            low = ref[0:SPAN, h * DH : (h + 1) * DH].astype(F32)
            high = ref[SPAN : 2 * SPAN, h * DH : (h + 1) * DH].astype(F32)
            even = jnp.where(last, low, high)
            odd = jnp.where(gone, 0.0, jnp.where(last, high, low))
            r0_ref[h, a] = jnp.where(t0 == 0, even, odd).astype(BF)
            r1_ref[h, a] = jnp.where(t0 == 0, odd, even).astype(BF)


def first_of(span, y_half):
    return jnp.clip(N_Z * y_half - span, 0, N_Z - 1)


def send_kernel(core, meta, k_ref, v_ref, out_ref, sem):
    blocks = pl.ds(first_of(meta[0], 1 - meta[1]), WINDOWS)

    @pl.when(meta[5] == core)
    def _():
        copies = [
            pltpu.make_async_copy(ref.at[blocks], out_ref.at[n], sem.at[n]) for n, ref in enumerate((k_ref, v_ref))
        ]
        for copy in copies:
            copy.start()
        for copy in copies:
            copy.wait()


def turn_kernel(meta, k_ref, v_ref, got0_ref, got1_ref, cos_ref, sin_ref, out_ref):
    cos, sin = cos_ref[...], sin_ref[...]

    def turn(x):
        x = x.astype(F32)
        return (x * cos + half_turn(x) * sin).astype(BF)

    for core, got_ref in enumerate((got0_ref, got1_ref)):

        @pl.when(meta[5] == core)
        def _():
            def step(w, carry):
                block = block_of(meta[0], meta[1], w)
                far = block - first_of(meta[0], meta[1])
                out_ref[w, 0] = turn(k_ref[block])
                out_ref[w, 1] = turn(got_ref[0, far])
                out_ref[w, 2] = v_ref[block]
                out_ref[w, 3] = got_ref[1, far]
                return carry

            lax.fori_loop(0, WINDOWS, step, 0)


def main_kernel(
    meta, len_ref, x_ref, kv_ref, qc_ref, qs_ref, kc_ref, ks_ref,
    out_hbm, local_hbm, send_hbm, out_ref, local_ref, send_ref, done_ref, out_sem, grad_sem,
):
    span, y_half, nbr = meta[0], meta[1], meta[2]
    qc, qs = qc_ref[...], qs_ref[...]
    kc, ks = kc_ref[...], ks_ref[...]
    lane = lax.broadcasted_iota(jnp.int32, (SPAN, NEIGH), 1)
    last = is_last()
    these = range(GROUP)
    each = [(i, n) for i in these for n in range(NBR)]

    def group(step, carry):
        places = [step * GROUP + i for i in these]
        slots = [jnp.minimum(w, WINDOWS - 1) for w in places]
        blocks = [block_of(span, y_half, w) for w in slots]

        def rows(w, a):
            body = jnp.where(w < N_Z, x_ref[place(jnp.minimum(w, N_Z - 1), span), a].astype(F32), 0.0)
            v = w - span
            edge = jnp.logical_and(v >= 0, v < N_Z)
            edge = jnp.where(edge, x_ref[place(jnp.clip(v, 0, N_Z - 1), span), a].astype(F32), 0.0)
            return jnp.where(last, edge, body)

        def live(i, n):
            unit = NBR * (2 * blocks[i] + span)
            return lane < len_ref[unit + (nbr if n == 0 else 1 - nbr)]

        keys = {(i, n): kv_ref[slots[i], n] for i, n in each}
        vals = {(i, n): kv_ref[slots[i], 2 + n] for i, n in each}
        q = [rows(w, 0) for w in places]
        gf = [rows(w, 1) for w in places]
        qw = [(x * qc + half_turn(x) * qs).astype(BF) for x in q]
        g = [x.astype(BF) for x in gf]
        s = {k: dot(qw[k[0]], keys[k], 1, 1) for k in each}
        gv = {k: dot(g[k[0]], vals[k], 1, 1) for k in each}
        s = {k: jnp.where(live(*k), s[k] * SCALE, -jnp.inf) for k in each}
        m = {k: jnp.max(s[k], axis=1, keepdims=True) for k in each}
        e = {k: jnp.exp(s[k] - m[k]) for k in each}
        total = {k: jnp.sum(e[k], axis=1, keepdims=True) for k in each}
        o = {k: dot(e[k].astype(BF), vals[k], 1, 0) for k in each}
        top = [jnp.maximum(m[i, 0], m[i, 1]) for i in these]
        part = {k: jnp.exp(m[k] - top[k[0]]) for k in each}
        inv = [1.0 / (part[i, 0] * total[i, 0] + part[i, 1] * total[i, 1]) for i in these]
        share = {k: part[k] * inv[k[0]] for k in each}
        att = [(share[i, 0] * o[i, 0] + share[i, 1] * o[i, 1]).astype(BF) for i in these]
        dots = [jnp.sum(gf[i] * att[i].astype(F32), axis=1, keepdims=True) for i in these]
        pr = {k: e[k] * share[k] for k in each}
        gs = {k: (pr[k] * (gv[k] - dots[k[0]]) * SCALE).astype(BF) for k in each}
        gq = {k: dot(gs[k], keys[k], 1, 0).astype(BF).astype(F32) for k in each}
        gq = [gq[i, 0] + gq[i, 1] for i in these]
        dk = {k: dot(gs[k], qw[k[0]], 0, 0) for k in each}
        dv = {k: dot(pr[k].astype(BF), g[k[0]], 0, 0).astype(BF) for k in each}
        dk = {k: (dk[k] * kc - half_turn(dk[k]) * ks).astype(BF) for k in each}
        for i, w in enumerate(places):
            done_ref[w, 0] = att[i]
            done_ref[w, 1] = (gq[i] * qc - half_turn(gq[i]) * qs).astype(BF)
            local_ref[w, 0] = dk[i, 0]
            local_ref[w, 1] = dv[i, 0]
            send_ref[w, 0] = dk[i, 1]
            send_ref[w, 1] = dv[i, 1]
        for copy in grads(step):
            copy.start()

        def whole(z, carry):
            for a in range(2):
                mine, edge = done_ref[z, a].astype(F32), done_ref[z + span, a].astype(F32)
                out_ref[z, a] = jnp.where(last, edge, mine).astype(BF)
            rows_out(z).start()
            return carry

        end = jnp.minimum(GROUP * (step + 1) - 1, N_Z)
        lax.fori_loop(jnp.maximum(GROUP * step - 1, 0), end, whole, 0)
        return carry

    def grads(step):
        these_slots = pl.ds(step * GROUP, GROUP)
        return [
            pltpu.make_async_copy(ref.at[these_slots], hbm.at[these_slots], grad_sem.at[step, n])
            for n, (ref, hbm) in enumerate(((local_ref, local_hbm), (send_ref, send_hbm)))
        ]

    def rows_out(z):
        return pltpu.make_async_copy(out_ref.at[z], out_hbm.at[place(z, span)], out_sem.at[z])

    lax.fori_loop(0, SLOTS // GROUP, group, 0)

    def finish(step, carry):
        for copy in grads(step):
            copy.wait()
        return carry

    lax.fori_loop(0, SLOTS // GROUP, finish, 0)

    def finish_rows(z, carry):
        rows_out(z).wait()
        return carry

    lax.fori_loop(0, N_Z, finish_rows, 0)


def settle_kernel(meta, local_ref, got_ref, gk_ref, gv_ref):
    span, y_half = meta[0], meta[1]

    def step(i, carry):
        mine, theirs = N_Z * y_half + i, N_Z * (1 - y_half) + i
        for n, ref in enumerate((gk_ref, gv_ref)):
            ref[mine] = local_ref[i + span, n]
            ref[theirs] = got_ref[i + span, n]
        return carry

    lax.fori_loop(0, N_Z, step, 0, unroll=4)

    @pl.when(span == 1)
    def _():
        mine, theirs = jnp.where(y_half == 0, N_Z, 0), jnp.where(y_half == 0, 0, N_Z)
        for n, ref in enumerate((gk_ref, gv_ref)):
            ref[N_Z - 1] = (local_ref[mine, n].astype(F32) + got_ref[theirs, n].astype(F32)).astype(BF)


def unpack_kernel(meta, r0_ref, r1_ref, att_ref, gq_ref):
    t0, ctx = meta[3], meta[4]
    last = is_last()
    gone = jnp.logical_and(ctx == 0, jnp.logical_not(last))
    for h in range(HEADS_HERE):
        for a, ref in enumerate((att_ref, gq_ref)):
            one = r0_ref[h, a].astype(F32)
            two = r1_ref[h, a].astype(F32)
            even = jnp.where(t0 == 0, one, two)
            odd = jnp.where(gone, 0.0, jnp.where(t0 == 0, two, one))
            ref[0:SPAN, h * DH : (h + 1) * DH] = jnp.where(last, even, odd).astype(BF)
            ref[SPAN : 2 * SPAN, h * DH : (h + 1) * DH] = jnp.where(last, odd, even).astype(BF)


def shaped(*shape):
    return jax.ShapeDtypeStruct(shape, BF)


def in_hbm(*shape):
    return pltpu.HBM(shape, BF)


def call(kernel, outs, n_vmem, flops=1000, moved=1000, **more):
    return pl.pallas_call(
        kernel,
        out_shape=outs,
        in_specs=[SMEM] + [VMEM] * n_vmem,
        out_specs=jax.tree.map(lambda _: VMEM, outs),
        compiler_params=pltpu.CompilerParams(vmem_limit_bytes=LIMIT),
        cost_estimate=pl.CostEstimate(flops=flops, bytes_accessed=moved, transcendentals=0),
        **more,
    )


def shards(queries, keys, values, cotangent, lengths):
    both = ("ctx", "tp")
    ctx, tp = lax.axis_index("ctx"), lax.axis_index("tp")
    span, nbr = tp // 2, tp % 2
    core = lax.axis_index("dp") % 2
    meta = jnp.stack([span, (ctx // N_Z) ^ nbr, nbr, tp % 2, ctx, core]).astype(jnp.int32)
    routes_out = routes()
    chunk = shaped(HEADS_HERE, 2, SPAN, DH)
    qc, qs = map(jnp.asarray, tables([*range(1, SPAN), 0]))
    kc, ks = map(jnp.asarray, tables(range(NEIGH)))
    swap = [(i, i ^ 1) for i in range(N_TP)]

    r0, r1 = call(pack_kernel, (chunk, chunk), 2, moved=1 << 20)(meta, queries[0], cotangent[0])
    pair = shaped(2, WINDOWS, NEIGH, DH)
    keys_here, values_here = keys.reshape(N_CTX, NEIGH, DH), values.reshape(N_CTX, NEIGH, DH)

    def swap_of(which, facts):
        sent = pl.pallas_call(
            functools.partial(send_kernel, which),
            out_shape=pair,
            in_specs=[SMEM, HBM, HBM],
            out_specs=VMEM,
            scratch_shapes=[pltpu.SemaphoreType.DMA((2,))],
            compiler_params=pltpu.CompilerParams(vmem_limit_bytes=LIMIT),
            cost_estimate=pl.CostEstimate(flops=0, bytes_accessed=2 << 20, transcendentals=0),
        )(facts, *(pltpu.with_memory_space_constraint(x, pltpu.HBM) for x in (keys_here, values_here)))
        pairs = [(N_DP * a + d, N_DP * b + d) for a, b in swap for d in (which, which + 2)]
        return lax.ppermute(sent, ("tp", "dp"), pairs)

    got1 = swap_of(1, meta)
    r0, r1, got1, meta_then = lax.optimization_barrier((r0, r1, got1, meta))
    r0 = lax.ppermute(r0, both, routes_out[0])
    r1 = lax.ppermute(r1, both, routes_out[1])
    got0 = swap_of(0, meta_then)
    turned = call(turn_kernel, shaped(WINDOWS, 4, NEIGH, DH), 6, flops=TURN_COST, moved=TURN_BYTES)(
        meta, keys_here, values_here, got0, got1, kc, ks
    )
    joined = jnp.concatenate([r0, r1], axis=0)
    rows = lax.all_to_all(joined, both, 0, 0, axis_index_groups=z_groups(), tiled=True)

    grads = shaped(SLOTS, 2, NEIGH, DH)
    row_set = (N_Z, 2, SPAN, DH)
    out, d_local, d_send = pl.pallas_call(
        main_kernel,
        out_shape=(in_hbm(*row_set), in_hbm(*grads.shape), in_hbm(*grads.shape)),
        in_specs=[SMEM, SMEM] + [VMEM] * 6,
        out_specs=(HBM,) * 3,
        scratch_shapes=[
            pltpu.VMEM(row_set, BF),
            pltpu.VMEM(grads.shape, BF),
            pltpu.VMEM(grads.shape, BF),
            pltpu.VMEM((SLOTS, 2, SPAN, DH), BF),
            pltpu.SemaphoreType.DMA((N_Z,)),
            pltpu.SemaphoreType.DMA((SLOTS // GROUP, 2)),
        ],
        compiler_params=pltpu.CompilerParams(vmem_limit_bytes=LIMIT),
        cost_estimate=pl.CostEstimate(flops=1 << 29, bytes_accessed=6 << 20, transcendentals=1 << 18),
    )(meta, lengths.reshape(-1), rows, turned, qc, qs, kc, ks)

    back = lax.all_to_all(out, both, 0, 0, axis_index_groups=z_groups(), tiled=True)
    d_got = lax.ppermute(d_send, "tp", swap)
    full = shaped(N_CTX, NEIGH, DH)
    gk, gv = call(settle_kernel, (full, full), 2, moved=4 << 20)(meta, d_local, d_got)

    r0 = lax.ppermute(back[:HEADS_HERE], both, turned_round(routes_out[0]))
    r1 = lax.ppermute(back[HEADS_HERE:], both, turned_round(routes_out[1]))
    wide = shaped(2 * SPAN, HEADS_HERE * DH)
    att, gq = call(unpack_kernel, (wide, wide), 2, moved=1 << 20)(meta, r0, r1)
    return att[None], gq[None], gk.reshape(keys.shape), gv.reshape(values.shape)


def solution(mesh):
    in_specs = (
        P("dp", "ctx", "tp"),
        P("dp", None, "tp", "ctx", None, None),
        P("dp", None, "tp", "ctx", None, None),
        P("dp", "ctx", "tp"),
        P("dp", None, None),
    )
    out_specs = (
        P("dp", "ctx", "tp"),
        P("dp", "ctx", "tp"),
        P("dp", None, "tp", "ctx", None, None),
        P("dp", None, "tp", "ctx", None, None),
    )
    return jax.shard_map(shards, mesh=mesh, in_specs=in_specs, out_specs=out_specs, check_vma=False)
```

```python
import functools
import math

import jax
import jax.numpy as jnp
import numpy as np
from jax import lax
from jax.experimental import pallas as pl
from jax.experimental.pallas import tpu as pltpu
from jax.sharding import PartitionSpec as P

DH = 128
SPAN = 64
NBR = 2
NEIGH = 128
N_Z = 16
N_CTX = 32
N_TP = 4
N_DP = 4
HEADS_HERE = 8
WINDOWS = N_Z + 1
GROUP = 6
SLOTS = 18
EARLY = 8
SCALE = 1.0 / math.sqrt(DH)
BF = jnp.bfloat16
F32 = jnp.float32
VMEM = pl.BlockSpec(memory_space=pltpu.VMEM)
SMEM = pl.BlockSpec(memory_space=pltpu.SMEM)
HBM = pl.BlockSpec(memory_space=pltpu.HBM)
LIMIT = 12 * 1024 * 1024
TURN_COST = 49 << 28
TURN_BYTES = 2 << 20


def flat(ctx, tp):
    return ctx * N_TP + tp


def worker(ctx, t1, span):
    return flat(N_Z * t1 + ctx % N_Z, 2 * span + ((ctx // N_Z) ^ t1))


def routes():
    return [
        [(flat(c, t), worker(c, t // 2, (t % 2) ^ k)) for c in range(N_CTX) for t in range(N_TP)]
        for k in range(2)
    ]


def turned_round(pairs):
    return [(b, a) for a, b in pairs]


def z_groups():
    groups = []
    for y in range(2):
        for t in range(N_TP):
            groups.append([flat(N_Z * y + (j ^ (8 * (t // 2))), t) for j in range(N_Z)])
    return groups


def tables(indices):
    freq = 10000.0 ** (-2.0 * np.arange(DH // 2, dtype=np.float64) / DH)
    angles = np.asarray(indices, np.float64)[:, None] * freq[None]
    cos, sin = np.cos(angles), np.sin(angles)
    return (
        np.concatenate([cos, cos], 1).astype(np.float32),
        np.concatenate([-sin, sin], 1).astype(np.float32),
    )


def half_turn(x):
    return pltpu.roll(x, DH // 2, 1)


def dot(a, b, da, db):
    return lax.dot_general(a, b, (((da,), (db,)), ((), ())), preferred_element_type=F32)


def block_of(span, y_half, w):
    return jnp.clip(N_Z * y_half - span + w, 0, N_CTX - 1)


def place(z, span):
    return lax.bitwise_xor(z, 8 * span)


def is_last():
    return lax.broadcasted_iota(jnp.int32, (SPAN, DH), 0) == SPAN - 1


def pack_kernel(meta, q_ref, g_ref, r0_ref, r1_ref):
    t0, ctx = meta[3], meta[4]
    last = is_last()
    gone = jnp.logical_and(ctx == 0, jnp.logical_not(last))
    for h in range(HEADS_HERE):
        for a, ref in enumerate((q_ref, g_ref)):
            low = ref[0:SPAN, h * DH : (h + 1) * DH].astype(F32)
            high = ref[SPAN : 2 * SPAN, h * DH : (h + 1) * DH].astype(F32)
            even = jnp.where(last, low, high)
            odd = jnp.where(gone, 0.0, jnp.where(last, high, low))
            r0_ref[h, a] = jnp.where(t0 == 0, even, odd).astype(BF)
            r1_ref[h, a] = jnp.where(t0 == 0, odd, even).astype(BF)


def first_of(span, y_half):
    return jnp.clip(N_Z * y_half - span, 0, N_Z - 1)


def first_send_kernel(core, meta, k_ref, v_ref, out_ref, sem):
    first = first_of(meta[0], 1 - meta[1])

    @pl.when(meta[5] == core)
    def _():
        copies = [
            pltpu.make_async_copy(k_ref.at[pl.ds(first, WINDOWS)], out_ref.at[pl.ds(0, WINDOWS)], sem.at[0]),
            pltpu.make_async_copy(v_ref.at[pl.ds(first, EARLY)], out_ref.at[pl.ds(WINDOWS, EARLY)], sem.at[1]),
        ]
        for copy in copies:
            copy.start()
        for copy in copies:
            copy.wait()


def last_send_kernel(meta, v_ref, out_ref, sem):
    first = first_of(meta[0], 1 - meta[1])
    copy = pltpu.make_async_copy(v_ref.at[pl.ds(first + EARLY, WINDOWS - EARLY)], out_ref, sem)
    copy.start()
    copy.wait()


def turn_kernel(meta, k_ref, v_ref, got0_ref, got1_ref, cos_ref, sin_ref, out_ref):
    cos, sin = cos_ref[...], sin_ref[...]

    def turn(x):
        x = x.astype(F32)
        return (x * cos + half_turn(x) * sin).astype(BF)

    for core, got_ref in enumerate((got0_ref, got1_ref)):

        @pl.when(meta[5] == core)
        def _():
            def step(w, carry):
                block = block_of(meta[0], meta[1], w)
                far = jnp.minimum(block - first_of(meta[0], meta[1]), WINDOWS - 1)
                out_ref[w, 0] = turn(k_ref[block])
                out_ref[w, 1] = turn(got_ref[far])
                out_ref[w, 2] = v_ref[block]
                out_ref[w, 3] = got_ref[WINDOWS + jnp.minimum(far, EARLY - 1)]
                return carry

            lax.fori_loop(0, SLOTS, step, 0)


def main_kernel(
    meta, len_ref, x_ref, kv_hbm, late_hbm, tab_hbm,
    out_hbm, local_hbm, send_hbm, late_ref, tab_ref, kv_ref, out_ref, local_ref, send_ref, done_ref, one_sem, kv_sem, out_sem, grad_sem,
):
    span, y_half, nbr = meta[0], meta[1], meta[2]
    lane = lax.broadcasted_iota(jnp.int32, (SPAN, NEIGH), 1)
    last = is_last()
    these = range(GROUP)
    each = [(i, n) for i in these for n in range(NBR)]

    def kv_in(step):
        slots = pl.ds(step * GROUP, GROUP)
        return pltpu.make_async_copy(kv_hbm.at[slots], kv_ref.at[slots], kv_sem.at[step])

    firsts = [
        pltpu.make_async_copy(tab_hbm, tab_ref, one_sem.at[0]),
        pltpu.make_async_copy(late_hbm, late_ref, one_sem.at[1]),
    ]
    firsts[0].start()
    kv_in(0).start()
    firsts[1].start()
    for step in range(1, SLOTS // GROUP):
        kv_in(step).start()
    for copy in firsts:
        copy.wait()
    qc, qs = tab_ref[0:SPAN], tab_ref[SPAN : 2 * SPAN]
    kc, ks = tab_ref[2 * SPAN : 2 * SPAN + NEIGH], tab_ref[2 * SPAN + NEIGH :]

    def group(step, carry):
        places = [step * GROUP + i for i in these]
        blocks = [block_of(span, y_half, w) for w in places]
        kv_in(step).wait()
        for w, block in zip(places, blocks):
            far = jnp.minimum(block - first_of(span, y_half), WINDOWS - 1)

            @pl.when(far >= EARLY)
            def _():
                kv_ref[w, 3] = late_ref[far - EARLY]


        def rows(w, a):
            body = jnp.where(w < N_Z, x_ref[place(jnp.minimum(w, N_Z - 1), span), a].astype(F32), 0.0)
            v = w - span
            edge = jnp.logical_and(v >= 0, v < N_Z)
            edge = jnp.where(edge, x_ref[place(jnp.clip(v, 0, N_Z - 1), span), a].astype(F32), 0.0)
            return jnp.where(last, edge, body)

        def live(i, n):
            unit = NBR * (2 * blocks[i] + span)
            return lane < len_ref[unit + (nbr if n == 0 else 1 - nbr)]

        keys = {(i, n): kv_ref[places[i], n] for i, n in each}
        vals = {(i, n): kv_ref[places[i], 2 + n] for i, n in each}
        q = [rows(w, 0) for w in places]
        gf = [rows(w, 1) for w in places]
        qw = [(x * qc + half_turn(x) * qs).astype(BF) for x in q]
        g = [x.astype(BF) for x in gf]
        s = {k: dot(qw[k[0]], keys[k], 1, 1) for k in each}
        gv = {k: dot(g[k[0]], vals[k], 1, 1) for k in each}
        s = {k: jnp.where(live(*k), s[k] * SCALE, -jnp.inf) for k in each}
        m = {k: jnp.max(s[k], axis=1, keepdims=True) for k in each}
        e = {k: jnp.exp(s[k] - m[k]) for k in each}
        total = {k: jnp.sum(e[k], axis=1, keepdims=True) for k in each}
        o = {k: dot(e[k].astype(BF), vals[k], 1, 0) for k in each}
        top = [jnp.maximum(m[i, 0], m[i, 1]) for i in these]
        part = {k: jnp.exp(m[k] - top[k[0]]) for k in each}
        inv = [1.0 / (part[i, 0] * total[i, 0] + part[i, 1] * total[i, 1]) for i in these]
        share = {k: part[k] * inv[k[0]] for k in each}
        att = [(share[i, 0] * o[i, 0] + share[i, 1] * o[i, 1]).astype(BF) for i in these]
        dots = [jnp.sum(gf[i] * att[i].astype(F32), axis=1, keepdims=True) for i in these]
        pr = {k: e[k] * share[k] for k in each}
        gs = {k: (pr[k] * (gv[k] - dots[k[0]]) * SCALE).astype(BF) for k in each}
        gq = {k: dot(gs[k], keys[k], 1, 0).astype(BF).astype(F32) for k in each}
        gq = [gq[i, 0] + gq[i, 1] for i in these]
        dk = {k: dot(gs[k], qw[k[0]], 0, 0) for k in each}
        dv = {k: dot(pr[k].astype(BF), g[k[0]], 0, 0).astype(BF) for k in each}
        dk = {k: (dk[k] * kc - half_turn(dk[k]) * ks).astype(BF) for k in each}
        for i, w in enumerate(places):
            done_ref[w, 0] = att[i]
            done_ref[w, 1] = (gq[i] * qc - half_turn(gq[i]) * qs).astype(BF)
            local_ref[w, 0] = dk[i, 0]
            local_ref[w, 1] = dv[i, 0]
            send_ref[w, 0] = dk[i, 1]
            send_ref[w, 1] = dv[i, 1]
        for copy in grads(step):
            copy.start()

        def whole(z, carry):
            for a in range(2):
                mine, edge = done_ref[z, a].astype(F32), done_ref[z + span, a].astype(F32)
                out_ref[z, a] = jnp.where(last, edge, mine).astype(BF)
            rows_out(z).start()
            return carry

        end = jnp.minimum(GROUP * (step + 1) - 1, N_Z)
        lax.fori_loop(jnp.maximum(GROUP * step - 1, 0), end, whole, 0)
        return carry

    def grads(step):
        these_slots = pl.ds(step * GROUP, GROUP)
        return [
            pltpu.make_async_copy(ref.at[these_slots], hbm.at[these_slots], grad_sem.at[step, n])
            for n, (ref, hbm) in enumerate(((local_ref, local_hbm), (send_ref, send_hbm)))
        ]

    def rows_out(z):
        return pltpu.make_async_copy(out_ref.at[z], out_hbm.at[place(z, span)], out_sem.at[z])

    lax.fori_loop(0, SLOTS // GROUP, group, 0)

    def finish(step, carry):
        for copy in grads(step):
            copy.wait()
        return carry

    lax.fori_loop(0, SLOTS // GROUP, finish, 0)

    def finish_rows(z, carry):
        rows_out(z).wait()
        return carry

    lax.fori_loop(0, N_Z, finish_rows, 0)


def settle_kernel(meta, local_ref, got_ref, gk_ref, gv_ref):
    span, y_half = meta[0], meta[1]

    def step(i, carry):
        mine, theirs = N_Z * y_half + i, N_Z * (1 - y_half) + i
        for n, ref in enumerate((gk_ref, gv_ref)):
            ref[mine] = local_ref[i + span, n]
            ref[theirs] = got_ref[i + span, n]
        return carry

    lax.fori_loop(0, N_Z, step, 0, unroll=4)

    @pl.when(span == 1)
    def _():
        mine, theirs = jnp.where(y_half == 0, N_Z, 0), jnp.where(y_half == 0, 0, N_Z)
        for n, ref in enumerate((gk_ref, gv_ref)):
            ref[N_Z - 1] = (local_ref[mine, n].astype(F32) + got_ref[theirs, n].astype(F32)).astype(BF)


def unpack_kernel(meta, r0_ref, r1_ref, att_ref, gq_ref):
    t0, ctx = meta[3], meta[4]
    last = is_last()
    gone = jnp.logical_and(ctx == 0, jnp.logical_not(last))
    for h in range(HEADS_HERE):
        for a, ref in enumerate((att_ref, gq_ref)):
            one = r0_ref[h, a].astype(F32)
            two = r1_ref[h, a].astype(F32)
            even = jnp.where(t0 == 0, one, two)
            odd = jnp.where(gone, 0.0, jnp.where(t0 == 0, two, one))
            ref[0:SPAN, h * DH : (h + 1) * DH] = jnp.where(last, even, odd).astype(BF)
            ref[SPAN : 2 * SPAN, h * DH : (h + 1) * DH] = jnp.where(last, odd, even).astype(BF)


def shaped(*shape):
    return jax.ShapeDtypeStruct(shape, BF)


def in_hbm(*shape):
    return pltpu.HBM(shape, BF)


def call(kernel, outs, n_vmem, flops=1000, moved=1000, **more):
    return pl.pallas_call(
        kernel,
        out_shape=outs,
        in_specs=[SMEM] + [VMEM] * n_vmem,
        out_specs=jax.tree.map(lambda _: VMEM, outs),
        compiler_params=pltpu.CompilerParams(vmem_limit_bytes=LIMIT),
        cost_estimate=pl.CostEstimate(flops=flops, bytes_accessed=moved, transcendentals=0),
        **more,
    )


def shards(queries, keys, values, cotangent, lengths):
    both = ("ctx", "tp")
    ctx, tp = lax.axis_index("ctx"), lax.axis_index("tp")
    span, nbr = tp // 2, tp % 2
    core = lax.axis_index("dp") % 2
    meta = jnp.stack([span, (ctx // N_Z) ^ nbr, nbr, tp % 2, ctx, core]).astype(jnp.int32)
    routes_out = routes()
    chunk = shaped(HEADS_HERE, 2, SPAN, DH)
    kc, ks = tables(range(NEIGH))
    tab = jnp.asarray(np.concatenate([*tables([*range(1, SPAN), 0]), kc, ks]))
    kc, ks = jnp.asarray(kc), jnp.asarray(ks)
    swap = [(i, i ^ 1) for i in range(N_TP)]

    r0, r1 = call(pack_kernel, (chunk, chunk), 2, moved=1 << 20)(meta, queries[0], cotangent[0])
    keys_here, values_here = keys.reshape(N_CTX, NEIGH, DH), values.reshape(N_CTX, NEIGH, DH)
    in_place = lambda x: pltpu.with_memory_space_constraint(x, pltpu.HBM)

    def sender(kernel, facts, arrays, blocks, sems):
        return pl.pallas_call(
            kernel,
            out_shape=shaped(blocks, NEIGH, DH),
            in_specs=[SMEM] + [HBM] * len(arrays),
            out_specs=VMEM,
            scratch_shapes=[sems],
            compiler_params=pltpu.CompilerParams(vmem_limit_bytes=LIMIT),
            cost_estimate=pl.CostEstimate(flops=0, bytes_accessed=2 << 20, transcendentals=0),
        )(facts, *map(in_place, arrays))

    def swap_of(which, facts):
        kernel = functools.partial(first_send_kernel, which)
        sent = sender(kernel, facts, (keys_here, values_here), WINDOWS + EARLY, pltpu.SemaphoreType.DMA((2,)))
        pairs = [(N_DP * a + d, N_DP * b + d) for a, b in swap for d in (which, which + 2)]
        return lax.ppermute(sent, ("tp", "dp"), pairs)

    got1 = swap_of(1, meta)
    r0, r1, got1, meta_then = lax.optimization_barrier((r0, r1, got1, meta))
    r0 = lax.ppermute(r0, both, routes_out[0])
    r1 = lax.ppermute(r1, both, routes_out[1])
    got0 = swap_of(0, meta_then)
    late = sender(last_send_kernel, meta_then, (values_here,), WINDOWS - EARLY, pltpu.SemaphoreType.DMA)
    late = lax.ppermute(late, "tp", swap)
    turned = call(turn_kernel, shaped(SLOTS, 4, NEIGH, DH), 6, flops=TURN_COST, moved=TURN_BYTES)(
        meta, keys_here, values_here, got0, got1, kc, ks
    )
    joined = jnp.concatenate([r0, r1], axis=0)
    rows = lax.all_to_all(joined, both, 0, 0, axis_index_groups=z_groups(), tiled=True)

    grads = shaped(SLOTS, 2, NEIGH, DH)
    row_set = (N_Z, 2, SPAN, DH)
    out, d_local, d_send = pl.pallas_call(
        main_kernel,
        out_shape=(in_hbm(*row_set), in_hbm(*grads.shape), in_hbm(*grads.shape)),
        in_specs=[SMEM, SMEM, VMEM, HBM, HBM, HBM],
        out_specs=(HBM,) * 3,
        scratch_shapes=[
            pltpu.VMEM((WINDOWS - EARLY, NEIGH, DH), BF),
            pltpu.VMEM(tab.shape, F32),
            pltpu.VMEM((SLOTS, 4, NEIGH, DH), BF),
            pltpu.VMEM(row_set, BF),
            pltpu.VMEM(grads.shape, BF),
            pltpu.VMEM(grads.shape, BF),
            pltpu.VMEM((SLOTS, 2, SPAN, DH), BF),
            pltpu.SemaphoreType.DMA((2,)),
            pltpu.SemaphoreType.DMA((SLOTS // GROUP,)),
            pltpu.SemaphoreType.DMA((N_Z,)),
            pltpu.SemaphoreType.DMA((SLOTS // GROUP, 2)),
        ],
        compiler_params=pltpu.CompilerParams(vmem_limit_bytes=LIMIT),
        cost_estimate=pl.CostEstimate(flops=1 << 29, bytes_accessed=6 << 20, transcendentals=1 << 18),
    )(meta, lengths.reshape(-1), rows, in_place(turned), in_place(late), in_place(tab))

    back = lax.all_to_all(out, both, 0, 0, axis_index_groups=z_groups(), tiled=True)
    d_got = lax.ppermute(d_send, "tp", swap)
    full = shaped(N_CTX, NEIGH, DH)
    gk, gv = call(settle_kernel, (full, full), 2, moved=4 << 20)(meta, d_local, d_got)

    r0 = lax.ppermute(back[:HEADS_HERE], both, turned_round(routes_out[0]))
    r1 = lax.ppermute(back[HEADS_HERE:], both, turned_round(routes_out[1]))
    wide = shaped(2 * SPAN, HEADS_HERE * DH)
    att, gq = call(unpack_kernel, (wide, wide), 2, moved=1 << 20)(meta, r0, r1)
    return att[None], gq[None], gk.reshape(keys.shape), gv.reshape(values.shape)


def solution(mesh):
    in_specs = (
        P("dp", "ctx", "tp"),
        P("dp", None, "tp", "ctx", None, None),
        P("dp", None, "tp", "ctx", None, None),
        P("dp", "ctx", "tp"),
        P("dp", None, None),
    )
    out_specs = (
        P("dp", "ctx", "tp"),
        P("dp", "ctx", "tp"),
        P("dp", None, "tp", "ctx", None, None),
        P("dp", None, "tp", "ctx", None, None),
    )
    return jax.shard_map(shards, mesh=mesh, in_specs=in_specs, out_specs=out_specs, check_vma=False)
```

```python
import functools
import math

import jax
import jax.numpy as jnp
import numpy as np
from jax import lax
from jax.experimental import pallas as pl
from jax.experimental.pallas import tpu as pltpu
from jax.sharding import PartitionSpec as P

DH = 128
SPAN = 64
NBR = 2
NEIGH = 128
N_Z = 16
N_CTX = 32
N_TP = 4
N_DP = 4
HEADS_HERE = 8
WINDOWS = N_Z + 1
GROUP = 6
SLOTS = 18
EARLY = 4
SCALE = 1.0 / math.sqrt(DH)
BF = jnp.bfloat16
F32 = jnp.float32
VMEM = pl.BlockSpec(memory_space=pltpu.VMEM)
SMEM = pl.BlockSpec(memory_space=pltpu.SMEM)
HBM = pl.BlockSpec(memory_space=pltpu.HBM)
LIMIT = 12 * 1024 * 1024
TURN_COST = 53 << 28
TURN_BYTES = 2 << 20


def flat(ctx, tp):
    return ctx * N_TP + tp


def worker(ctx, t1, span):
    return flat(N_Z * t1 + ctx % N_Z, 2 * span + ((ctx // N_Z) ^ t1))


def routes():
    return [
        [(flat(c, t), worker(c, t // 2, (t % 2) ^ k)) for c in range(N_CTX) for t in range(N_TP)]
        for k in range(2)
    ]


def turned_round(pairs):
    return [(b, a) for a, b in pairs]


def z_groups():
    groups = []
    for y in range(2):
        for t in range(N_TP):
            groups.append([flat(N_Z * y + (j ^ (8 * (t // 2))), t) for j in range(N_Z)])
    return groups


def tables(indices):
    freq = 10000.0 ** (-2.0 * np.arange(DH // 2, dtype=np.float64) / DH)
    angles = np.asarray(indices, np.float64)[:, None] * freq[None]
    cos, sin = np.cos(angles), np.sin(angles)
    return (
        np.concatenate([cos, cos], 1).astype(np.float32),
        np.concatenate([-sin, sin], 1).astype(np.float32),
    )


def half_turn(x):
    return pltpu.roll(x, DH // 2, 1)


def dot(a, b, da, db):
    return lax.dot_general(a, b, (((da,), (db,)), ((), ())), preferred_element_type=F32)


def block_of(span, y_half, w):
    return jnp.clip(N_Z * y_half - span + w, 0, N_CTX - 1)


def place(z, span):
    return lax.bitwise_xor(z, 8 * span)


def is_last():
    return lax.broadcasted_iota(jnp.int32, (SPAN, DH), 0) == SPAN - 1


def pack_kernel(meta, q_ref, g_ref, r0_ref, r1_ref):
    t0, ctx = meta[3], meta[4]
    last = is_last()
    gone = jnp.logical_and(ctx == 0, jnp.logical_not(last))
    for h in range(HEADS_HERE):
        for a, ref in enumerate((q_ref, g_ref)):
            low = ref[0:SPAN, h * DH : (h + 1) * DH].astype(F32)
            high = ref[SPAN : 2 * SPAN, h * DH : (h + 1) * DH].astype(F32)
            even = jnp.where(last, low, high)
            odd = jnp.where(gone, 0.0, jnp.where(last, high, low))
            r0_ref[h, a] = jnp.where(t0 == 0, even, odd).astype(BF)
            r1_ref[h, a] = jnp.where(t0 == 0, odd, even).astype(BF)


def first_of(span, y_half):
    return jnp.clip(N_Z * y_half - span, 0, N_Z - 1)


def first_send_kernel(core, meta, k_ref, v_ref, out_ref, sem):
    first = first_of(meta[0], 1 - meta[1])

    @pl.when(meta[5] == core)
    def _():
        copies = [
            pltpu.make_async_copy(k_ref.at[pl.ds(first, WINDOWS)], out_ref.at[pl.ds(0, WINDOWS)], sem.at[0]),
            pltpu.make_async_copy(v_ref.at[pl.ds(first, EARLY)], out_ref.at[pl.ds(WINDOWS, EARLY)], sem.at[1]),
        ]
        for copy in copies:
            copy.start()
        for copy in copies:
            copy.wait()


def last_send_kernel(meta, v_ref, out_ref, sem):
    first = first_of(meta[0], 1 - meta[1])
    copy = pltpu.make_async_copy(v_ref.at[pl.ds(first + EARLY, WINDOWS - EARLY)], out_ref, sem)
    copy.start()
    copy.wait()


def turn_kernel(meta, k_ref, v_ref, got0_ref, got1_ref, cos_ref, sin_ref, out_ref):
    cos, sin = cos_ref[...], sin_ref[...]

    def turn(x):
        x = x.astype(F32)
        return (x * cos + half_turn(x) * sin).astype(BF)

    for core, got_ref in enumerate((got0_ref, got1_ref)):

        @pl.when(meta[5] == core)
        def _():
            def step(w, carry):
                block = block_of(meta[0], meta[1], w)
                far = jnp.minimum(block - first_of(meta[0], meta[1]), WINDOWS - 1)
                out_ref[w, 0] = turn(k_ref[block])
                out_ref[w, 1] = turn(got_ref[far])
                out_ref[w, 2] = v_ref[block]
                out_ref[w, 3] = got_ref[WINDOWS + jnp.minimum(far, EARLY - 1)]
                return carry

            lax.fori_loop(0, SLOTS, step, 0)


def main_kernel(
    meta, len_ref, x_ref, kv_hbm, late_hbm, tab_hbm,
    out_hbm, local_hbm, send_hbm, late_ref, tab_ref, kv_ref, out_ref, local_ref, send_ref, done_ref, one_sem, kv_sem, out_sem, grad_sem,
):
    span, y_half, nbr = meta[0], meta[1], meta[2]
    lane = lax.broadcasted_iota(jnp.int32, (SPAN, NEIGH), 1)
    last = is_last()
    these = range(GROUP)
    each = [(i, n) for i in these for n in range(NBR)]

    def kv_in(step):
        slots = pl.ds(step * GROUP, GROUP)
        return pltpu.make_async_copy(kv_hbm.at[slots], kv_ref.at[slots], kv_sem.at[step])

    firsts = [
        pltpu.make_async_copy(tab_hbm, tab_ref, one_sem.at[0]),
        pltpu.make_async_copy(late_hbm, late_ref, one_sem.at[1]),
    ]
    firsts[0].start()
    kv_in(0).start()
    firsts[1].start()
    for step in range(1, SLOTS // GROUP):
        kv_in(step).start()
    for copy in firsts:
        copy.wait()
    qc, qs = tab_ref[0:SPAN], tab_ref[SPAN : 2 * SPAN]
    kc, ks = tab_ref[2 * SPAN : 2 * SPAN + NEIGH], tab_ref[2 * SPAN + NEIGH :]

    def group(step, carry):
        places = [step * GROUP + i for i in these]
        blocks = [block_of(span, y_half, w) for w in places]
        kv_in(step).wait()
        for w, block in zip(places, blocks):
            far = jnp.minimum(block - first_of(span, y_half), WINDOWS - 1)

            @pl.when(far >= EARLY)
            def _():
                kv_ref[w, 3] = late_ref[far - EARLY]


        def rows(w, a):
            body = jnp.where(w < N_Z, x_ref[place(jnp.minimum(w, N_Z - 1), span), a].astype(F32), 0.0)
            v = w - span
            edge = jnp.logical_and(v >= 0, v < N_Z)
            edge = jnp.where(edge, x_ref[place(jnp.clip(v, 0, N_Z - 1), span), a].astype(F32), 0.0)
            return jnp.where(last, edge, body)

        def live(i, n):
            unit = NBR * (2 * blocks[i] + span)
            return lane < len_ref[unit + (nbr if n == 0 else 1 - nbr)]

        keys = {(i, n): kv_ref[places[i], n] for i, n in each}
        vals = {(i, n): kv_ref[places[i], 2 + n] for i, n in each}
        q = [rows(w, 0) for w in places]
        gf = [rows(w, 1) for w in places]
        qw = [(x * qc + half_turn(x) * qs).astype(BF) for x in q]
        g = [x.astype(BF) for x in gf]
        s = {k: dot(qw[k[0]], keys[k], 1, 1) for k in each}
        gv = {k: dot(g[k[0]], vals[k], 1, 1) for k in each}
        s = {k: jnp.where(live(*k), s[k] * SCALE, -jnp.inf) for k in each}
        m = {k: jnp.max(s[k], axis=1, keepdims=True) for k in each}
        e = {k: jnp.exp(s[k] - m[k]) for k in each}
        total = {k: jnp.sum(e[k], axis=1, keepdims=True) for k in each}
        o = {k: dot(e[k].astype(BF), vals[k], 1, 0) for k in each}
        top = [jnp.maximum(m[i, 0], m[i, 1]) for i in these]
        part = {k: jnp.exp(m[k] - top[k[0]]) for k in each}
        inv = [1.0 / (part[i, 0] * total[i, 0] + part[i, 1] * total[i, 1]) for i in these]
        share = {k: part[k] * inv[k[0]] for k in each}
        att = [(share[i, 0] * o[i, 0] + share[i, 1] * o[i, 1]).astype(BF) for i in these]
        dots = [jnp.sum(gf[i] * att[i].astype(F32), axis=1, keepdims=True) for i in these]
        pr = {k: e[k] * share[k] for k in each}
        gs = {k: (pr[k] * (gv[k] - dots[k[0]]) * SCALE).astype(BF) for k in each}
        gq = {k: dot(gs[k], keys[k], 1, 0).astype(BF).astype(F32) for k in each}
        gq = [gq[i, 0] + gq[i, 1] for i in these]
        dk = {k: dot(gs[k], qw[k[0]], 0, 0) for k in each}
        dv = {k: dot(pr[k].astype(BF), g[k[0]], 0, 0).astype(BF) for k in each}
        dk = {k: (dk[k] * kc - half_turn(dk[k]) * ks).astype(BF) for k in each}
        for i, w in enumerate(places):
            done_ref[w, 0] = att[i]
            done_ref[w, 1] = (gq[i] * qc - half_turn(gq[i]) * qs).astype(BF)
            local_ref[w, 0] = dk[i, 0]
            local_ref[w, 1] = dv[i, 0]
            send_ref[w, 0] = dk[i, 1]
            send_ref[w, 1] = dv[i, 1]
        for copy in grads(step):
            copy.start()

        def whole(z, carry):
            for a in range(2):
                mine, edge = done_ref[z, a].astype(F32), done_ref[z + span, a].astype(F32)
                out_ref[z, a] = jnp.where(last, edge, mine).astype(BF)
            rows_out(z).start()
            return carry

        end = jnp.minimum(GROUP * (step + 1) - 1, N_Z)
        lax.fori_loop(jnp.maximum(GROUP * step - 1, 0), end, whole, 0)
        return carry

    def grads(step):
        these_slots = pl.ds(step * GROUP, GROUP)
        return [
            pltpu.make_async_copy(ref.at[these_slots], hbm.at[these_slots], grad_sem.at[step, n])
            for n, (ref, hbm) in enumerate(((local_ref, local_hbm), (send_ref, send_hbm)))
        ]

    def rows_out(z):
        return pltpu.make_async_copy(out_ref.at[z], out_hbm.at[place(z, span)], out_sem.at[z])

    lax.fori_loop(0, SLOTS // GROUP, group, 0)

    def finish(step, carry):
        for copy in grads(step):
            copy.wait()
        return carry

    lax.fori_loop(0, SLOTS // GROUP, finish, 0)

    def finish_rows(z, carry):
        rows_out(z).wait()
        return carry

    lax.fori_loop(0, N_Z, finish_rows, 0)


def settle_kernel(meta, local_ref, got_ref, gk_ref, gv_ref):
    span, y_half = meta[0], meta[1]

    def step(i, carry):
        mine, theirs = N_Z * y_half + i, N_Z * (1 - y_half) + i
        for n, ref in enumerate((gk_ref, gv_ref)):
            ref[mine] = local_ref[i + span, n]
            ref[theirs] = got_ref[i + span, n]
        return carry

    lax.fori_loop(0, N_Z, step, 0, unroll=4)

    @pl.when(span == 1)
    def _():
        mine, theirs = jnp.where(y_half == 0, N_Z, 0), jnp.where(y_half == 0, 0, N_Z)
        for n, ref in enumerate((gk_ref, gv_ref)):
            ref[N_Z - 1] = (local_ref[mine, n].astype(F32) + got_ref[theirs, n].astype(F32)).astype(BF)


def unpack_kernel(meta, r0_ref, r1_ref, att_ref, gq_ref):
    t0, ctx = meta[3], meta[4]
    last = is_last()
    gone = jnp.logical_and(ctx == 0, jnp.logical_not(last))
    for h in range(HEADS_HERE):
        for a, ref in enumerate((att_ref, gq_ref)):
            one = r0_ref[h, a].astype(F32)
            two = r1_ref[h, a].astype(F32)
            even = jnp.where(t0 == 0, one, two)
            odd = jnp.where(gone, 0.0, jnp.where(t0 == 0, two, one))
            ref[0:SPAN, h * DH : (h + 1) * DH] = jnp.where(last, even, odd).astype(BF)
            ref[SPAN : 2 * SPAN, h * DH : (h + 1) * DH] = jnp.where(last, odd, even).astype(BF)


def shaped(*shape):
    return jax.ShapeDtypeStruct(shape, BF)


def in_hbm(*shape):
    return pltpu.HBM(shape, BF)


def call(kernel, outs, n_vmem, flops=1000, moved=1000, **more):
    return pl.pallas_call(
        kernel,
        out_shape=outs,
        in_specs=[SMEM] + [VMEM] * n_vmem,
        out_specs=jax.tree.map(lambda _: VMEM, outs),
        compiler_params=pltpu.CompilerParams(vmem_limit_bytes=LIMIT),
        cost_estimate=pl.CostEstimate(flops=flops, bytes_accessed=moved, transcendentals=0),
        **more,
    )


def shards(queries, keys, values, cotangent, lengths):
    both = ("ctx", "tp")
    ctx, tp = lax.axis_index("ctx"), lax.axis_index("tp")
    span, nbr = tp // 2, tp % 2
    core = lax.axis_index("dp") % 2
    meta = jnp.stack([span, (ctx // N_Z) ^ nbr, nbr, tp % 2, ctx, core]).astype(jnp.int32)
    routes_out = routes()
    chunk = shaped(HEADS_HERE, 2, SPAN, DH)
    kc, ks = tables(range(NEIGH))
    tab = jnp.asarray(np.concatenate([*tables([*range(1, SPAN), 0]), kc, ks]))
    kc, ks = jnp.asarray(kc), jnp.asarray(ks)
    swap = [(i, i ^ 1) for i in range(N_TP)]

    r0, r1 = call(pack_kernel, (chunk, chunk), 2, moved=1 << 20)(meta, queries[0], cotangent[0])
    keys_here, values_here = keys.reshape(N_CTX, NEIGH, DH), values.reshape(N_CTX, NEIGH, DH)
    in_place = lambda x: pltpu.with_memory_space_constraint(x, pltpu.HBM)

    def sender(kernel, facts, arrays, blocks, sems):
        return pl.pallas_call(
            kernel,
            out_shape=shaped(blocks, NEIGH, DH),
            in_specs=[SMEM] + [HBM] * len(arrays),
            out_specs=VMEM,
            scratch_shapes=[sems],
            compiler_params=pltpu.CompilerParams(vmem_limit_bytes=LIMIT),
            cost_estimate=pl.CostEstimate(flops=0, bytes_accessed=2 << 20, transcendentals=0),
        )(facts, *map(in_place, arrays))

    def swap_of(which, facts):
        kernel = functools.partial(first_send_kernel, which)
        sent = sender(kernel, facts, (keys_here, values_here), WINDOWS + EARLY, pltpu.SemaphoreType.DMA((2,)))
        pairs = [(N_DP * a + d, N_DP * b + d) for a, b in swap for d in (which, which + 2)]
        return lax.ppermute(sent, ("tp", "dp"), pairs)

    got1 = swap_of(1, meta)
    r0, r1, got1, meta_then = lax.optimization_barrier((r0, r1, got1, meta))
    r0 = lax.ppermute(r0, both, routes_out[0])
    r1 = lax.ppermute(r1, both, routes_out[1])
    got0 = swap_of(0, meta_then)
    late = sender(last_send_kernel, meta_then, (values_here,), WINDOWS - EARLY, pltpu.SemaphoreType.DMA)
    late = lax.ppermute(late, "tp", swap)
    turned = call(turn_kernel, shaped(SLOTS, 4, NEIGH, DH), 6, flops=TURN_COST, moved=TURN_BYTES)(
        meta, keys_here, values_here, got0, got1, kc, ks
    )
    joined = jnp.concatenate([r0, r1], axis=0)
    rows = lax.all_to_all(joined, both, 0, 0, axis_index_groups=z_groups(), tiled=True)

    grads = shaped(SLOTS, 2, NEIGH, DH)
    row_set = (N_Z, 2, SPAN, DH)
    out, d_local, d_send = pl.pallas_call(
        main_kernel,
        out_shape=(in_hbm(*row_set), in_hbm(*grads.shape), in_hbm(*grads.shape)),
        in_specs=[SMEM, SMEM, VMEM, HBM, HBM, HBM],
        out_specs=(HBM,) * 3,
        scratch_shapes=[
            pltpu.VMEM((WINDOWS - EARLY, NEIGH, DH), BF),
            pltpu.VMEM(tab.shape, F32),
            pltpu.VMEM((SLOTS, 4, NEIGH, DH), BF),
            pltpu.VMEM(row_set, BF),
            pltpu.VMEM(grads.shape, BF),
            pltpu.VMEM(grads.shape, BF),
            pltpu.VMEM((SLOTS, 2, SPAN, DH), BF),
            pltpu.SemaphoreType.DMA((2,)),
            pltpu.SemaphoreType.DMA((SLOTS // GROUP,)),
            pltpu.SemaphoreType.DMA((N_Z,)),
            pltpu.SemaphoreType.DMA((SLOTS // GROUP, 2)),
        ],
        compiler_params=pltpu.CompilerParams(vmem_limit_bytes=LIMIT),
        cost_estimate=pl.CostEstimate(flops=1 << 29, bytes_accessed=6 << 20, transcendentals=1 << 18),
    )(meta, lengths.reshape(-1), rows, in_place(turned), in_place(late), in_place(tab))

    back = lax.all_to_all(out, both, 0, 0, axis_index_groups=z_groups(), tiled=True)
    d_got = lax.ppermute(d_send, "tp", swap)
    full = shaped(N_CTX, NEIGH, DH)
    gk, gv = call(settle_kernel, (full, full), 2, moved=4 << 20)(meta, d_local, d_got)

    r0 = lax.ppermute(back[:HEADS_HERE], both, turned_round(routes_out[0]))
    r1 = lax.ppermute(back[HEADS_HERE:], both, turned_round(routes_out[1]))
    wide = shaped(2 * SPAN, HEADS_HERE * DH)
    att, gq = call(unpack_kernel, (wide, wide), 2, moved=1 << 20)(meta, r0, r1)
    return att[None], gq[None], gk.reshape(keys.shape), gv.reshape(values.shape)


def solution(mesh):
    in_specs = (
        P("dp", "ctx", "tp"),
        P("dp", None, "tp", "ctx", None, None),
        P("dp", None, "tp", "ctx", None, None),
        P("dp", "ctx", "tp"),
        P("dp", None, None),
    )
    out_specs = (
        P("dp", "ctx", "tp"),
        P("dp", "ctx", "tp"),
        P("dp", None, "tp", "ctx", None, None),
        P("dp", None, "tp", "ctx", None, None),
    )
    return jax.shard_map(shards, mesh=mesh, in_specs=in_specs, out_specs=out_specs, check_vma=False)
```

```python
import functools
import math

import jax
import jax.numpy as jnp
import numpy as np
from jax import lax
from jax.experimental import pallas as pl
from jax.experimental.pallas import tpu as pltpu
from jax.sharding import PartitionSpec as P

DH = 128
SPAN = 64
NBR = 2
NEIGH = 128
N_Z = 16
N_CTX = 32
N_TP = 4
N_DP = 4
HEADS_HERE = 8
WINDOWS = N_Z + 1
GROUP = 6
SLOTS = 18
EARLY = 10
SCALE = 1.0 / math.sqrt(DH)
BF = jnp.bfloat16
F32 = jnp.float32
VMEM = pl.BlockSpec(memory_space=pltpu.VMEM)
SMEM = pl.BlockSpec(memory_space=pltpu.SMEM)
HBM = pl.BlockSpec(memory_space=pltpu.HBM)
LIMIT = 12 * 1024 * 1024
TURN_COST = 49 << 28
TURN_BYTES = 2 << 20


def flat(ctx, tp):
    return ctx * N_TP + tp


def worker(ctx, t1, span):
    return flat(N_Z * t1 + ctx % N_Z, 2 * span + ((ctx // N_Z) ^ t1))


def routes():
    return [
        [(flat(c, t), worker(c, t // 2, (t % 2) ^ k)) for c in range(N_CTX) for t in range(N_TP)]
        for k in range(2)
    ]


def turned_round(pairs):
    return [(b, a) for a, b in pairs]


def z_groups():
    groups = []
    for y in range(2):
        for t in range(N_TP):
            groups.append([flat(N_Z * y + (j ^ (8 * (t // 2))), t) for j in range(N_Z)])
    return groups


def tables(indices):
    freq = 10000.0 ** (-2.0 * np.arange(DH // 2, dtype=np.float64) / DH)
    angles = np.asarray(indices, np.float64)[:, None] * freq[None]
    cos, sin = np.cos(angles), np.sin(angles)
    return (
        np.concatenate([cos, cos], 1).astype(np.float32),
        np.concatenate([-sin, sin], 1).astype(np.float32),
    )


def half_turn(x):
    return pltpu.roll(x, DH // 2, 1)


def dot(a, b, da, db):
    return lax.dot_general(a, b, (((da,), (db,)), ((), ())), preferred_element_type=F32)


def block_of(span, y_half, w):
    return jnp.clip(N_Z * y_half - span + w, 0, N_CTX - 1)


def place(z, span):
    return lax.bitwise_xor(z, 8 * span)


def is_last():
    return lax.broadcasted_iota(jnp.int32, (SPAN, DH), 0) == SPAN - 1


def pack_kernel(meta, q_ref, g_ref, r0_ref, r1_ref):
    t0, ctx = meta[3], meta[4]
    last = is_last()
    gone = jnp.logical_and(ctx == 0, jnp.logical_not(last))
    for h in range(HEADS_HERE):
        for a, ref in enumerate((q_ref, g_ref)):
            low = ref[0:SPAN, h * DH : (h + 1) * DH].astype(F32)
            high = ref[SPAN : 2 * SPAN, h * DH : (h + 1) * DH].astype(F32)
            even = jnp.where(last, low, high)
            odd = jnp.where(gone, 0.0, jnp.where(last, high, low))
            r0_ref[h, a] = jnp.where(t0 == 0, even, odd).astype(BF)
            r1_ref[h, a] = jnp.where(t0 == 0, odd, even).astype(BF)


def first_of(span, y_half):
    return jnp.clip(N_Z * y_half - span, 0, N_Z - 1)


def first_send_kernel(core, meta, k_ref, v_ref, out_ref, sem):
    first = first_of(meta[0], 1 - meta[1])

    @pl.when(meta[5] == core)
    def _():
        copies = [
            pltpu.make_async_copy(k_ref.at[pl.ds(first, WINDOWS)], out_ref.at[pl.ds(0, WINDOWS)], sem.at[0]),
            pltpu.make_async_copy(v_ref.at[pl.ds(first, EARLY)], out_ref.at[pl.ds(WINDOWS, EARLY)], sem.at[1]),
        ]
        for copy in copies:
            copy.start()
        for copy in copies:
            copy.wait()


def last_send_kernel(meta, v_ref, out_ref, sem):
    first = first_of(meta[0], 1 - meta[1])
    copy = pltpu.make_async_copy(v_ref.at[pl.ds(first + EARLY, WINDOWS - EARLY)], out_ref, sem)
    copy.start()
    copy.wait()


def turn_kernel(meta, k_ref, v_ref, got0_ref, got1_ref, cos_ref, sin_ref, out_ref):
    cos, sin = cos_ref[...], sin_ref[...]

    def turn(x):
        x = x.astype(F32)
        return (x * cos + half_turn(x) * sin).astype(BF)

    for core, got_ref in enumerate((got0_ref, got1_ref)):

        @pl.when(meta[5] == core)
        def _():
            def step(w, carry):
                block = block_of(meta[0], meta[1], w)
                far = jnp.minimum(block - first_of(meta[0], meta[1]), WINDOWS - 1)
                out_ref[w, 0] = turn(k_ref[block])
                out_ref[w, 1] = turn(got_ref[far])
                out_ref[w, 2] = v_ref[block]
                out_ref[w, 3] = got_ref[WINDOWS + jnp.minimum(far, EARLY - 1)]
                return carry

            lax.fori_loop(0, SLOTS, step, 0)


def main_kernel(
    meta, len_ref, x_ref, kv_hbm, late_hbm, tab_hbm,
    out_hbm, local_hbm, send_hbm, late_ref, tab_ref, kv_ref, out_ref, local_ref, send_ref, done_ref, one_sem, kv_sem, out_sem, grad_sem,
):
    span, y_half, nbr = meta[0], meta[1], meta[2]
    lane = lax.broadcasted_iota(jnp.int32, (SPAN, NEIGH), 1)
    last = is_last()
    these = range(GROUP)
    each = [(i, n) for i in these for n in range(NBR)]

    def kv_in(step):
        slots = pl.ds(step * GROUP, GROUP)
        return pltpu.make_async_copy(kv_hbm.at[slots], kv_ref.at[slots], kv_sem.at[step])

    firsts = [
        pltpu.make_async_copy(tab_hbm, tab_ref, one_sem.at[0]),
        pltpu.make_async_copy(late_hbm, late_ref, one_sem.at[1]),
    ]
    firsts[0].start()
    kv_in(0).start()
    firsts[1].start()
    for step in range(1, SLOTS // GROUP):
        kv_in(step).start()
    for copy in firsts:
        copy.wait()
    qc, qs = tab_ref[0:SPAN], tab_ref[SPAN : 2 * SPAN]
    kc, ks = tab_ref[2 * SPAN : 2 * SPAN + NEIGH], tab_ref[2 * SPAN + NEIGH :]

    def group(step, carry):
        places = [step * GROUP + i for i in these]
        blocks = [block_of(span, y_half, w) for w in places]
        kv_in(step).wait()
        for w, block in zip(places, blocks):
            far = jnp.minimum(block - first_of(span, y_half), WINDOWS - 1)

            @pl.when(far >= EARLY)
            def _():
                kv_ref[w, 3] = late_ref[far - EARLY]


        def rows(w, a):
            body = jnp.where(w < N_Z, x_ref[place(jnp.minimum(w, N_Z - 1), span), a].astype(F32), 0.0)
            v = w - span
            edge = jnp.logical_and(v >= 0, v < N_Z)
            edge = jnp.where(edge, x_ref[place(jnp.clip(v, 0, N_Z - 1), span), a].astype(F32), 0.0)
            return jnp.where(last, edge, body)

        def live(i, n):
            unit = NBR * (2 * blocks[i] + span)
            return lane < len_ref[unit + (nbr if n == 0 else 1 - nbr)]

        keys = {(i, n): kv_ref[places[i], n] for i, n in each}
        vals = {(i, n): kv_ref[places[i], 2 + n] for i, n in each}
        q = [rows(w, 0) for w in places]
        gf = [rows(w, 1) for w in places]
        qw = [(x * qc + half_turn(x) * qs).astype(BF) for x in q]
        g = [x.astype(BF) for x in gf]
        s = {k: dot(qw[k[0]], keys[k], 1, 1) for k in each}
        gv = {k: dot(g[k[0]], vals[k], 1, 1) for k in each}
        s = {k: jnp.where(live(*k), s[k] * SCALE, -jnp.inf) for k in each}
        m = {k: jnp.max(s[k], axis=1, keepdims=True) for k in each}
        e = {k: jnp.exp(s[k] - m[k]) for k in each}
        total = {k: jnp.sum(e[k], axis=1, keepdims=True) for k in each}
        o = {k: dot(e[k].astype(BF), vals[k], 1, 0) for k in each}
        top = [jnp.maximum(m[i, 0], m[i, 1]) for i in these]
        part = {k: jnp.exp(m[k] - top[k[0]]) for k in each}
        inv = [1.0 / (part[i, 0] * total[i, 0] + part[i, 1] * total[i, 1]) for i in these]
        share = {k: part[k] * inv[k[0]] for k in each}
        att = [(share[i, 0] * o[i, 0] + share[i, 1] * o[i, 1]).astype(BF) for i in these]
        dots = [jnp.sum(gf[i] * att[i].astype(F32), axis=1, keepdims=True) for i in these]
        pr = {k: e[k] * share[k] for k in each}
        gs = {k: (pr[k] * (gv[k] - dots[k[0]]) * SCALE).astype(BF) for k in each}
        gq = {k: dot(gs[k], keys[k], 1, 0).astype(BF).astype(F32) for k in each}
        gq = [gq[i, 0] + gq[i, 1] for i in these]
        dk = {k: dot(gs[k], qw[k[0]], 0, 0) for k in each}
        dv = {k: dot(pr[k].astype(BF), g[k[0]], 0, 0).astype(BF) for k in each}
        dk = {k: (dk[k] * kc - half_turn(dk[k]) * ks).astype(BF) for k in each}
        for i, w in enumerate(places):
            done_ref[w, 0] = att[i]
            done_ref[w, 1] = (gq[i] * qc - half_turn(gq[i]) * qs).astype(BF)
            local_ref[w, 0] = dk[i, 0]
            local_ref[w, 1] = dv[i, 0]
            send_ref[w, 0] = dk[i, 1]
            send_ref[w, 1] = dv[i, 1]
        for copy in grads(step):
            copy.start()

        def whole(z, carry):
            for a in range(2):
                mine, edge = done_ref[z, a].astype(F32), done_ref[z + span, a].astype(F32)
                out_ref[z, a] = jnp.where(last, edge, mine).astype(BF)
            rows_out(z).start()
            return carry

        end = jnp.minimum(GROUP * (step + 1) - 1, N_Z)
        lax.fori_loop(jnp.maximum(GROUP * step - 1, 0), end, whole, 0)
        return carry

    def grads(step):
        these_slots = pl.ds(step * GROUP, GROUP)
        return [
            pltpu.make_async_copy(ref.at[these_slots], hbm.at[these_slots], grad_sem.at[step, n])
            for n, (ref, hbm) in enumerate(((local_ref, local_hbm), (send_ref, send_hbm)))
        ]

    def rows_out(z):
        return pltpu.make_async_copy(out_ref.at[z], out_hbm.at[place(z, span)], out_sem.at[z])

    lax.fori_loop(0, SLOTS // GROUP, group, 0)

    def finish(step, carry):
        for copy in grads(step):
            copy.wait()
        return carry

    lax.fori_loop(0, SLOTS // GROUP, finish, 0)

    def finish_rows(z, carry):
        rows_out(z).wait()
        return carry

    lax.fori_loop(0, N_Z, finish_rows, 0)


def settle_kernel(meta, local_ref, got_ref, gk_ref, gv_ref):
    span, y_half = meta[0], meta[1]

    def step(i, carry):
        mine, theirs = N_Z * y_half + i, N_Z * (1 - y_half) + i
        for n, ref in enumerate((gk_ref, gv_ref)):
            ref[mine] = local_ref[i + span, n]
            ref[theirs] = got_ref[i + span, n]
        return carry

    lax.fori_loop(0, N_Z, step, 0, unroll=4)

    @pl.when(span == 1)
    def _():
        mine, theirs = jnp.where(y_half == 0, N_Z, 0), jnp.where(y_half == 0, 0, N_Z)
        for n, ref in enumerate((gk_ref, gv_ref)):
            ref[N_Z - 1] = (local_ref[mine, n].astype(F32) + got_ref[theirs, n].astype(F32)).astype(BF)


def unpack_kernel(meta, r0_ref, r1_ref, att_ref, gq_ref):
    t0, ctx = meta[3], meta[4]
    last = is_last()
    gone = jnp.logical_and(ctx == 0, jnp.logical_not(last))
    for h in range(HEADS_HERE):
        for a, ref in enumerate((att_ref, gq_ref)):
            one = r0_ref[h, a].astype(F32)
            two = r1_ref[h, a].astype(F32)
            even = jnp.where(t0 == 0, one, two)
            odd = jnp.where(gone, 0.0, jnp.where(t0 == 0, two, one))
            ref[0:SPAN, h * DH : (h + 1) * DH] = jnp.where(last, even, odd).astype(BF)
            ref[SPAN : 2 * SPAN, h * DH : (h + 1) * DH] = jnp.where(last, odd, even).astype(BF)


def shaped(*shape):
    return jax.ShapeDtypeStruct(shape, BF)


def in_hbm(*shape):
    return pltpu.HBM(shape, BF)


def call(kernel, outs, n_vmem, flops=1000, moved=1000, **more):
    return pl.pallas_call(
        kernel,
        out_shape=outs,
        in_specs=[SMEM] + [VMEM] * n_vmem,
        out_specs=jax.tree.map(lambda _: VMEM, outs),
        compiler_params=pltpu.CompilerParams(vmem_limit_bytes=LIMIT),
        cost_estimate=pl.CostEstimate(flops=flops, bytes_accessed=moved, transcendentals=0),
        **more,
    )


def shards(queries, keys, values, cotangent, lengths):
    both = ("ctx", "tp")
    ctx, tp = lax.axis_index("ctx"), lax.axis_index("tp")
    span, nbr = tp // 2, tp % 2
    core = lax.axis_index("dp") % 2
    meta = jnp.stack([span, (ctx // N_Z) ^ nbr, nbr, tp % 2, ctx, core]).astype(jnp.int32)
    routes_out = routes()
    chunk = shaped(HEADS_HERE, 2, SPAN, DH)
    kc, ks = tables(range(NEIGH))
    tab = jnp.asarray(np.concatenate([*tables([*range(1, SPAN), 0]), kc, ks]))
    kc, ks = jnp.asarray(kc), jnp.asarray(ks)
    swap = [(i, i ^ 1) for i in range(N_TP)]

    r0, r1 = call(pack_kernel, (chunk, chunk), 2, moved=1 << 20)(meta, queries[0], cotangent[0])
    keys_here, values_here = keys.reshape(N_CTX, NEIGH, DH), values.reshape(N_CTX, NEIGH, DH)
    in_place = lambda x: pltpu.with_memory_space_constraint(x, pltpu.HBM)

    def sender(kernel, facts, arrays, blocks, sems):
        return pl.pallas_call(
            kernel,
            out_shape=shaped(blocks, NEIGH, DH),
            in_specs=[SMEM] + [HBM] * len(arrays),
            out_specs=VMEM,
            scratch_shapes=[sems],
            compiler_params=pltpu.CompilerParams(vmem_limit_bytes=LIMIT),
            cost_estimate=pl.CostEstimate(flops=0, bytes_accessed=2 << 20, transcendentals=0),
        )(facts, *map(in_place, arrays))

    def swap_of(which, facts):
        kernel = functools.partial(first_send_kernel, which)
        sent = sender(kernel, facts, (keys_here, values_here), WINDOWS + EARLY, pltpu.SemaphoreType.DMA((2,)))
        pairs = [(N_DP * a + d, N_DP * b + d) for a, b in swap for d in (which, which + 2)]
        return lax.ppermute(sent, ("tp", "dp"), pairs)

    got1 = swap_of(1, meta)
    r0, r1, got1, meta_then = lax.optimization_barrier((r0, r1, got1, meta))
    r0 = lax.ppermute(r0, both, routes_out[0])
    r1 = lax.ppermute(r1, both, routes_out[1])
    got0 = swap_of(0, meta_then)
    late = sender(last_send_kernel, meta_then, (values_here,), WINDOWS - EARLY, pltpu.SemaphoreType.DMA)
    late = lax.ppermute(late, "tp", swap)
    turned = call(turn_kernel, shaped(SLOTS, 4, NEIGH, DH), 6, flops=TURN_COST, moved=TURN_BYTES)(
        meta, keys_here, values_here, got0, got1, kc, ks
    )
    joined = jnp.concatenate([r0, r1], axis=0)
    rows = lax.all_to_all(joined, both, 0, 0, axis_index_groups=z_groups(), tiled=True)

    grads = shaped(SLOTS, 2, NEIGH, DH)
    row_set = (N_Z, 2, SPAN, DH)
    out, d_local, d_send = pl.pallas_call(
        main_kernel,
        out_shape=(in_hbm(*row_set), in_hbm(*grads.shape), in_hbm(*grads.shape)),
        in_specs=[SMEM, SMEM, VMEM, HBM, HBM, HBM],
        out_specs=(HBM,) * 3,
        scratch_shapes=[
            pltpu.VMEM((WINDOWS - EARLY, NEIGH, DH), BF),
            pltpu.VMEM(tab.shape, F32),
            pltpu.VMEM((SLOTS, 4, NEIGH, DH), BF),
            pltpu.VMEM(row_set, BF),
            pltpu.VMEM(grads.shape, BF),
            pltpu.VMEM(grads.shape, BF),
            pltpu.VMEM((SLOTS, 2, SPAN, DH), BF),
            pltpu.SemaphoreType.DMA((2,)),
            pltpu.SemaphoreType.DMA((SLOTS // GROUP,)),
            pltpu.SemaphoreType.DMA((N_Z,)),
            pltpu.SemaphoreType.DMA((SLOTS // GROUP, 2)),
        ],
        compiler_params=pltpu.CompilerParams(vmem_limit_bytes=LIMIT),
        cost_estimate=pl.CostEstimate(flops=1 << 29, bytes_accessed=6 << 20, transcendentals=1 << 18),
    )(meta, lengths.reshape(-1), rows, in_place(turned), in_place(late), in_place(tab))

    back = lax.all_to_all(out, both, 0, 0, axis_index_groups=z_groups(), tiled=True)
    d_got = lax.ppermute(d_send, "tp", swap)
    full = shaped(N_CTX, NEIGH, DH)
    gk, gv = call(settle_kernel, (full, full), 2, moved=4 << 20)(meta, d_local, d_got)

    r0 = lax.ppermute(back[:HEADS_HERE], both, turned_round(routes_out[0]))
    r1 = lax.ppermute(back[HEADS_HERE:], both, turned_round(routes_out[1]))
    wide = shaped(2 * SPAN, HEADS_HERE * DH)
    att, gq = call(unpack_kernel, (wide, wide), 2, moved=1 << 20)(meta, r0, r1)
    return att[None], gq[None], gk.reshape(keys.shape), gv.reshape(values.shape)


def solution(mesh):
    in_specs = (
        P("dp", "ctx", "tp"),
        P("dp", None, "tp", "ctx", None, None),
        P("dp", None, "tp", "ctx", None, None),
        P("dp", "ctx", "tp"),
        P("dp", None, None),
    )
    out_specs = (
        P("dp", "ctx", "tp"),
        P("dp", "ctx", "tp"),
        P("dp", None, "tp", "ctx", None, None),
        P("dp", None, "tp", "ctx", None, None),
    )
    return jax.shard_map(shards, mesh=mesh, in_specs=in_specs, out_specs=out_specs, check_vma=False)
```
